32 devices in a mesh: freq: 16 (over z, x, core), space: 2 (over y).
Axes of the slice: x: 2, y: 2, z: 4, core: 2. Of those that a mesh axis runs over, the one named last changes fastest.
Arguments:
- series: bfloat16 [2048, 32768], P('freq', 'space')
- starts: int32 [7], replicated, may hold values from 0 to 1536, as said below
- freqs: int32 [16], replicated, may hold values from 0 to 511, as said below
- alpha: int32 [1], replicated, may hold values from 1 to 63
Outputs:
- spectra: bfloat16 [16, 2, 7, 32768], P('freq', None, None, 'space')
- gram: float32 [16, 2, 63, 63], P('freq')
The draws below stay inside these ranges and needn't reach their ends.
Inputs may be any that keep to these rules, and one draw needn't show every extreme that they name: `starts`: increasing; the first is 0, the last 1536; consecutive ones lie 512 / 4 to 384 apart. `freqs`: 16 distinct bins, 0 and 511 among them.
All inputs are finite; a program needn't handle non-finite values.
Results may differ from the reference program's by a relative error of at most 0.005.
Values may be sent and summed in bfloat16 or wider, within the bound.
A program may use at most 64 MiB of HBM per device.

```python
import math
import jax
import jax.numpy as jnp
from jax import lax

NFFT = 512
NBLK = 7
HALF = 4
C_SP = 16384
SHIFTS = 9
NT = 2048
CELLS = 32768
NFREQ = 16
N_SPACE = 2


def draw_series(key, part):
    keys = jax.random.split(key, 6)
    position = jnp.arange(CELLS, dtype=jnp.float32) / CELLS
    rough = jnp.exp(jax.random.uniform(keys[0], (CELLS,), jnp.float32, -0.1, 0.1))
    amplitude = jnp.sqrt(1.0 + 2.0 * position) * rough / 2.2
    noise = jax.random.normal(keys[1], (NT, CELLS), jnp.float32)
    common_weight = 0.8
    signals = jax.random.normal(keys[2], (3, NT, 1), jnp.float32)
    fields = jax.random.normal(keys[3], (3, 1, CELLS), jnp.float32)
    common = signals[0] * fields[0] + signals[1] * fields[1] + signals[2] * fields[2]
    tone_bins = jax.random.randint(keys[4], (CELLS,), 0, NFFT).astype(jnp.int32)
    tone_start = jax.random.uniform(keys[5], (CELLS,), jnp.float32, -math.pi, math.pi)
    time_index = jnp.arange(NT, dtype=jnp.int32)
    tone_steps = jnp.mod(time_index[:, None] * tone_bins[None, :], NFFT).astype(jnp.float32)
    tone = 2.0 * jnp.cos(tone_steps * (2.0 * math.pi / NFFT) + tone_start[None, :])
    values = amplitude[None, :] * (noise + common_weight * common + tone)
    return jnp.clip(values, -40.0, 40.0).astype(jnp.bfloat16)


def draw_starts(key, part):
    hop_size = NFFT // 2
    jitter = jax.random.randint(key, (NBLK,), -(hop_size // 4), hop_size // 4 + 1)
    nominal = jnp.arange(NBLK, dtype=jnp.int32) * hop_size
    block_index = jnp.arange(NBLK, dtype=jnp.int32)
    inner = (block_index > 0) & (block_index < NBLK - 1)
    return jnp.where(inner, nominal + jitter, nominal).astype(jnp.int32)


def draw_freqs(key, part):
    pick_key = jax.random.fold_in(key, 11)
    order_key = jax.random.fold_in(key, 23)
    inner_bins = jax.random.permutation(pick_key, NFFT - 2)[:NFREQ - 2].astype(jnp.int32) + 1
    ends = jnp.array([0, NFFT - 1], dtype=jnp.int32)
    chosen = jnp.concatenate([ends, inner_bins])
    placing = jax.random.permutation(order_key, NFREQ)
    return chosen[placing].astype(jnp.int32)


def setup_inputs(seed: int = 0) -> dict:
    key_list = jax.random.split(jax.random.key(seed), 5)
    series = draw_series(jax.random.fold_in(key_list[4], 71), 0)
    starts = draw_starts(jax.random.fold_in(key_list[4], 71), 0)
    freqs = draw_freqs(jax.random.fold_in(key_list[4], 71), 0)
    alpha = jax.random.randint(key_list[3], (1,), 1, NFFT // 8).astype(jnp.int32)
    return {"series": series, "starts": starts, "freqs": freqs, "alpha": alpha}


def transform_table(freqs, alpha):
    sample_index = jnp.arange(NFFT, dtype=jnp.int32)
    shift_index = jnp.arange(SHIFTS, dtype=jnp.int32) - HALF
    freq_bins = jnp.mod(freqs[:, None] + shift_index[None, :] * alpha[0], NFFT).astype(jnp.int32)
    phase_steps = jnp.mod(freq_bins[:, :, None] * sample_index[None, None, :], NFFT)
    phase = phase_steps.astype(jnp.float32) * (2.0 * math.pi / NFFT)
    sample_float = sample_index.astype(jnp.float32)
    window_shape = 0.5 - 0.5 * jnp.cos(sample_float * (2.0 * math.pi / NFFT))
    window_scale = window_shape / jnp.sqrt(jnp.sum(window_shape * window_shape))
    real_part = window_scale * jnp.cos(phase)
    imag_part = -(window_scale * jnp.sin(phase))
    return jnp.stack([real_part, imag_part], axis=1).astype(jnp.bfloat16)

def split_quadrants(products, order):
    real_gram = products[..., :order, :order] + products[..., order:, order:]
    imag_gram = products[..., :order, order:] - products[..., order:, :order]
    return jnp.stack([real_gram, imag_gram], axis=-3)

def reference(series, starts, freqs, alpha):
    table = transform_table(freqs, alpha)
    nfreq = freqs.shape[0]
    order = SHIFTS * NBLK
    flat_table = table.reshape(nfreq * 2 * SHIFTS, NFFT).astype(jnp.float32)

    def one_slab(carry, slab_index):
        cell_rows = lax.dynamic_slice_in_dim(series, (slab_index * C_SP).astype(jnp.int32), C_SP, 1)
        blocks = []
        for block in range(NBLK):
            block_rows = lax.dynamic_slice_in_dim(cell_rows, starts[block].astype(jnp.int32), NFFT, 0)
            spec_block = jnp.dot(flat_table, block_rows.astype(jnp.float32), precision=lax.Precision.HIGHEST)
            blocks.append(spec_block.astype(jnp.bfloat16).reshape(nfreq, 2, SHIFTS, C_SP))
        blockspec = jnp.stack(blocks, axis=3)
        stacked = blockspec.reshape(nfreq, 2 * order, C_SP).astype(jnp.float32)
        products = jnp.einsum('jrc,jsc->jrs', stacked, stacked, precision=lax.Precision.HIGHEST)
        return (carry + split_quadrants(products, order), blockspec[:, :, HALF])
    initial = jnp.zeros((nfreq, 2, order, order), jnp.float32)
    summed, own_slabs = lax.scan(one_slab, initial, jnp.arange(N_SPACE, dtype=jnp.int32))
    spectra = jnp.transpose(own_slabs, (1, 2, 3, 0, 4)).reshape(nfreq, 2, NBLK, N_SPACE * C_SP)
    gram = summed / (C_SP * N_SPACE)
    return (spectra, gram)
```

```python
import math

import jax
import jax.numpy as jnp
from jax import lax
from jax.sharding import PartitionSpec as P

NFFT = 512
NBLK = 7
HALF = 4
SHIFTS = 9


def transform_table(freqs, alpha):
    sample_index = jnp.arange(NFFT, dtype=jnp.int32)
    shift_index = jnp.arange(SHIFTS, dtype=jnp.int32) - HALF
    freq_bins = jnp.mod(freqs[:, None] + shift_index[None, :] * alpha[0], NFFT)
    phase_steps = jnp.mod(freq_bins[:, :, None] * sample_index[None, None, :], NFFT)
    phase = phase_steps.astype(jnp.float32) * (2.0 * math.pi / NFFT)
    sample_float = sample_index.astype(jnp.float32)
    window_shape = 0.5 - 0.5 * jnp.cos(sample_float * (2.0 * math.pi / NFFT))
    window_scale = window_shape / jnp.sqrt(jnp.sum(window_shape * window_shape))
    real_part = window_scale * jnp.cos(phase)
    imag_part = -(window_scale * jnp.sin(phase))
    return jnp.stack([real_part, imag_part], axis=1).astype(jnp.bfloat16)


def split_quadrants(products, order):
    real_gram = products[..., :order, :order] + products[..., order:, order:]
    imag_gram = products[..., :order, order:] - products[..., order:, :order]
    return jnp.stack([real_gram, imag_gram], axis=-3)


def per_device(series, starts, freqs, alpha):
    slab_cells = series.shape[1]
    total_cells = slab_cells * lax.axis_size("space")
    nfreq = freqs.shape[0]
    order = SHIFTS * NBLK
    local_rows = lax.all_to_all(series, "freq", split_axis=1, concat_axis=0, tiled=True)
    local_cells = local_rows.shape[1]
    flat_table = transform_table(freqs, alpha).reshape(nfreq * 2 * SHIFTS, NFFT)
    blocks = []
    for block in range(NBLK):
        block_rows = lax.dynamic_slice_in_dim(local_rows, starts[block], NFFT, 0)
        spec_block = jnp.dot(flat_table, block_rows, preferred_element_type=jnp.float32)
        blocks.append(spec_block.astype(jnp.bfloat16).reshape(nfreq, 2, SHIFTS, local_cells))
    blockspec = jnp.stack(blocks, axis=3)
    own_spectra = lax.all_to_all(
        blockspec[:, :, HALF], "freq", split_axis=0, concat_axis=3, tiled=True
    )
    stacked = blockspec.reshape(nfreq, 2 * order, local_cells)
    products = lax.dot_general(
        stacked, stacked, (((2,), (2,)), ((0,), (0,))), preferred_element_type=jnp.float32
    )
    gram_part = split_quadrants(products, order)
    gram_own = lax.psum_scatter(gram_part, "freq", scatter_dimension=0, tiled=True)
    gram = lax.psum(gram_own, "space") / total_cells
    return (own_spectra, gram)


def solution(mesh):
    placed = (P("freq", "space"), P(), P(), P())
    return jax.shard_map(
        per_device,
        mesh=mesh,
        in_specs=placed,
        out_specs=(P("freq", None, None, "space"), P("freq", None, None, None)),
        check_vma=False,
    )
```

```python
import functools
import math

import jax
import jax.numpy as jnp
from jax import lax
from jax.experimental import pallas as pl
from jax.experimental.pallas import tpu as pltpu
from jax.sharding import PartitionSpec as P

NFFT = 512
NBLK = 7
HALF = 4
SHIFTS = 9
ORDER = SHIFTS * NBLK
QUAD = 64
GRAM_ROWS = 2 * QUAD
OWN_ROWS = 16
FREQ_ROWS = GRAM_ROWS + OWN_ROWS
GROUP = 4
MESH = pl.DeviceIdType.MESH


def half_turn_sine(steps):
    x = steps.astype(jnp.float32) * (math.pi / 256.0)
    x2 = x * x
    p = -1.0 / math.factorial(11)
    for order in (9, 7, 5, 3, 1):
        p = p * x2 + (-1.0) ** ((order - 1) // 2) / math.factorial(order)
    return p * x


def negative_cosine(step):
    folded = 128 - jnp.abs((step & (NFFT - 1)) - NFFT // 2)
    return half_turn_sine(folded)


def row_fields(starts):
    row = lax.broadcasted_iota(jnp.int32, (FREQ_ROWS, 128), 0)
    own = row >= GRAM_ROWS
    half = jnp.where(own, GRAM_ROWS + OWN_ROWS // 2, QUAD)
    part = jnp.where(row >= half, 1, 0)
    inner = jnp.where(own, row - GRAM_ROWS - OWN_ROWS // 2 * part, row - QUAD * part)
    shift = jnp.zeros_like(row)
    for bound in range(1, SHIFTS + 1):
        shift += jnp.where(inner >= NBLK * bound, 1, 0)
    block = jnp.where(own, inner, inner - NBLK * shift)
    used = inner < jnp.where(own, NBLK, ORDER)
    shift = jnp.where(own, HALF, shift)
    first = jnp.zeros_like(row)
    for index in range(NBLK):
        first = jnp.where(block == index, starts[index], first)
    return shift, part, first, used


def kernel(
    n,
    ns,
    nfreq,
    nchunk,
    total_cells,
    starts_ref,
    freqs_ref,
    alpha_ref,
    series_ref,
    spec_ref,
    gram_ref,
    table,
    weight,
    elapsed,
    spread,
    stage,
    accum,
    pack_out,
    pack_in,
    space_parts,
    raw_send,
    raw_recv,
    spec_send,
    spec_recv,
    gram_send,
    gram_recv,
    space_send,
    space_recv,
    local_sem,
    *slabs,
):
    me = lax.axis_index("freq")
    my_space = lax.axis_index("space")
    rows, slab_cells = series_ref.shape
    nt = rows * n
    own_cells = slab_cells // n
    width = own_cells // nchunk

    def at_freq(peer):
        return {"freq": peer, "space": my_space}

    def at_space(peer):
        return {"freq": me, "space": peer}

    barrier = pltpu.get_barrier_semaphore()

    @pl.loop(1, n)
    def _(k):
        pl.semaphore_signal(
            barrier, inc=1, device_id=at_freq(lax.rem(me + k, n)), device_id_type=MESH
        )

    @pl.loop(1, ns)
    def _(k):
        pl.semaphore_signal(
            barrier, inc=1, device_id=at_space(lax.rem(my_space + k, ns)), device_id_type=MESH
        )

    pl.semaphore_wait(barrier, n + ns - 2)

    def raw_copy(c, peer, slot):
        cells = pl.ds(pl.multiple_of(peer * own_cells + c * width, 128), width)
        mine = pl.ds(pl.multiple_of(me * rows, rows), rows)
        return pltpu.make_async_remote_copy(
            src_ref=series_ref.at[:, cells],
            dst_ref=slabs[c].at[mine, :],
            send_sem=raw_send.at[c, peer],
            recv_sem=raw_recv.at[c, slot],
            device_id=at_freq(peer),
            device_id_type=MESH,
        )

    def own_copy(c):
        cells = pl.ds(pl.multiple_of(me * own_cells + c * width, 128), width)
        mine = pl.ds(pl.multiple_of(me * rows, rows), rows)
        return pltpu.make_async_copy(
            series_ref.at[:, cells], slabs[c].at[mine, :], local_sem.at[0, c]
        )

    def spec_copy(c, peer, slot):
        cells = pl.ds(pl.multiple_of(me * own_cells + c * width, 128), width)
        return pltpu.make_async_remote_copy(
            src_ref=stage.at[c, peer],
            dst_ref=spec_ref.at[:, cells],
            send_sem=spec_send.at[c, peer],
            recv_sem=spec_recv.at[c, slot],
            device_id=at_freq(peer),
            device_id_type=MESH,
        )

    def own_spec_copy(c):
        cells = pl.ds(pl.multiple_of(me * own_cells + c * width, 128), width)
        return pltpu.make_async_copy(
            stage.at[c, me], spec_ref.at[:, cells], local_sem.at[1, c]
        )

    def gram_copy(peer, slot):
        return pltpu.make_async_remote_copy(
            src_ref=pack_out.at[peer],
            dst_ref=pack_in.at[me],
            send_sem=gram_send.at[peer],
            recv_sem=gram_recv.at[slot],
            device_id=at_freq(peer),
            device_id_type=MESH,
        )

    def space_copy(peer, slot):
        return pltpu.make_async_remote_copy(
            src_ref=space_parts.at[my_space],
            dst_ref=space_parts.at[my_space],
            send_sem=space_send.at[peer],
            recv_sem=space_recv.at[slot],
            device_id=at_space(peer),
            device_id_type=MESH,
        )

    for c in range(nchunk):

        @pl.loop(1, n)
        def _(k):
            raw_copy(c, lax.rem(me + k, n), me).start()

        own_copy(c).start()

    shift, part, first, used = row_fields([starts_ref[b] for b in range(NBLK)])
    quarter = part * (NFFT // 4)
    scale = 0.5 / math.sqrt(0.375 * NFFT)
    lane = lax.broadcasted_iota(jnp.int32, (FREQ_ROWS, 128), 1)

    @pl.loop(0, nt // 128)
    def _(i):
        cols = pl.ds(pl.multiple_of(i * 128, 128), 128)
        t = lane + i * 128 - first
        inside = (t >= 0) & (t < NFFT) & used
        window = scale + scale * negative_cosine(t)
        elapsed[:, cols] = t
        weight[:, cols] = jnp.where(inside, -window, 0.0)

    @pl.loop(0, nfreq)
    def _(j):
        bins = freqs_ref[j] + (shift - HALF) * alpha_ref[0]
        base = pl.multiple_of(j * FREQ_ROWS, 16)

        @pl.loop(0, nt // 128)
        def _(i):
            cols = pl.ds(pl.multiple_of(i * 128, 128), 128)
            step = bins * elapsed[:, cols] + quarter
            value = negative_cosine(step) * weight[:, cols]
            table[pl.ds(base, FREQ_ROWS), cols] = value.astype(jnp.bfloat16)

    for c in range(nchunk):
        own_copy(c).wait()

        @pl.loop(1, n)
        def _(k):
            peer = lax.rem(me + k, n)
            raw_copy(c, peer, peer).wait_recv()

        @pl.loop(0, nfreq // GROUP)
        def _(g):
            base = pl.multiple_of(g * (GROUP * FREQ_ROWS), 16)
            result = jnp.dot(
                table[pl.ds(base, GROUP * FREQ_ROWS), :],
                slabs[c][...],
                preferred_element_type=jnp.float32,
            ).astype(jnp.bfloat16)
            for i in range(GROUP):
                j = g * GROUP + i
                spread[j] = result[i * FREQ_ROWS : i * FREQ_ROWS + GRAM_ROWS]
                stage[c, j] = result[i * FREQ_ROWS + GRAM_ROWS : (i + 1) * FREQ_ROWS]

        @pl.loop(1, n)
        def _(k):
            peer = lax.rem(me + k, n)
            spec_copy(c, peer, me).start()

        own_spec_copy(c).start()

        @pl.loop(0, nfreq)
        def _(j):
            lines = spread[j]
            product = lax.dot_general(
                lines, lines, (((1,), (1,)), ((), ())), preferred_element_type=jnp.float32
            )
            if c == 0:
                accum[j] = product
            else:
                accum[j] += product

    prow = lax.broadcasted_iota(jnp.int32, (QUAD, 128), 0)
    pcol = lax.broadcasted_iota(jnp.int32, (QUAD, 128), 1)
    left = lax.broadcasted_iota(jnp.int32, (QUAD // 2, 128), 1) < QUAD

    @pl.loop(0, nfreq)
    def _(j):
        whole = accum[j]
        turned = pltpu.roll(whole, QUAD, 1)
        real = whole[:QUAD] + turned[QUAD:]
        imag = turned[:QUAD] - whole[QUAD:]
        mixed = jnp.where(prow <= pcol, real, imag)
        low = pltpu.roll(mixed[QUAD // 2 :], QUAD, 1)
        pack_out[j] = jnp.where(left, mixed[: QUAD // 2], low).astype(jnp.bfloat16)

    pack_in[me] = pack_out[me]

    @pl.loop(1, n)
    def _(k):
        gram_copy(lax.rem(me + k, n), me).start()

    @pl.loop(1, n)
    def _(k):
        peer = lax.rem(me + k, n)
        gram_copy(peer, peer).wait_recv()

    total = pack_in[0].astype(jnp.float32)
    for p in range(1, n):
        total += pack_in[p].astype(jnp.float32)
    space_parts[my_space] = total

    @pl.loop(1, ns)
    def _(k):
        space_copy(lax.rem(my_space + k, ns), my_space).start()

    @pl.loop(1, ns)
    def _(k):
        peer = lax.rem(my_space + k, ns)
        pltpu.make_async_remote_copy(
            src_ref=space_parts.at[my_space],
            dst_ref=space_parts.at[peer],
            send_sem=space_send.at[peer],
            recv_sem=space_recv.at[peer],
            device_id=at_space(peer),
            device_id_type=MESH,
        ).wait_recv()

    total = space_parts[0]
    for p in range(1, ns):
        total += space_parts[p]
    total = total * (1.0 / total_cells)
    mixed = jnp.concatenate(
        [total, pltpu.roll(total, QUAD, 1), jnp.zeros((QUAD, 128), jnp.float32)], axis=0
    )
    flipped = mixed.T[:QUAD]
    mixed = mixed[:QUAD]
    real = jnp.where(prow <= pcol, mixed, flipped)
    imag = jnp.where(prow > pcol, mixed, jnp.where(prow == pcol, 0.0, -flipped))
    gram_ref[0, 0] = real[:ORDER, :ORDER]
    gram_ref[0, 1] = imag[:ORDER, :ORDER]

    for c in range(nchunk):
        own_spec_copy(c).wait()

        @pl.loop(1, n)
        def _(k):
            peer = lax.rem(me + k, n)
            spec_copy(c, peer, peer).wait_recv()

    for c in range(nchunk):

        @pl.loop(1, n)
        def _(k):
            peer = lax.rem(me + k, n)
            raw_copy(c, peer, me).wait_send()
            spec_copy(c, peer, me).wait_send()

    @pl.loop(1, n)
    def _(k):
        peer = lax.rem(me + k, n)
        gram_copy(peer, me).wait_send()

    @pl.loop(1, ns)
    def _(k):
        space_copy(lax.rem(my_space + k, ns), my_space).wait_send()


def solution(mesh):
    n = mesh.shape["freq"]
    ns = mesh.shape["space"]

    def per_device(series, starts, freqs, alpha):
        rows, slab_cells = series.shape
        nfreq = freqs.shape[0]
        nt = rows * n
        own_cells = slab_cells // n
        nchunk = max(2, own_cells // 256)
        width = own_cells // nchunk
        smem = pl.BlockSpec(memory_space=pltpu.SMEM)
        table_rows = nfreq * FREQ_ROWS
        cost = pl.CostEstimate(
            flops=2 * table_rows * nt * own_cells,
            bytes_accessed=2 * rows * slab_cells * 2,
            transcendentals=0,
        )
        dma = pltpu.SemaphoreType.DMA
        spec, gram = pl.pallas_call(
            functools.partial(kernel, n, ns, nfreq, nchunk, slab_cells * ns),
            out_shape=(
                jax.ShapeDtypeStruct((OWN_ROWS, slab_cells), jnp.bfloat16),
                jax.ShapeDtypeStruct((1, 2, ORDER, ORDER), jnp.float32),
            ),
            in_specs=[smem, smem, smem, pl.BlockSpec(memory_space=pl.ANY)],
            out_specs=(
                pl.BlockSpec(memory_space=pl.ANY),
                pl.BlockSpec(memory_space=pltpu.VMEM),
            ),
            scratch_shapes=[
                pltpu.VMEM((table_rows, nt), jnp.bfloat16),
                pltpu.VMEM((FREQ_ROWS, nt), jnp.float32),
                pltpu.VMEM((FREQ_ROWS, nt), jnp.int32),
                pltpu.VMEM((nfreq, GRAM_ROWS, width), jnp.bfloat16),
                pltpu.VMEM((nchunk, nfreq, OWN_ROWS, width), jnp.bfloat16),
                pltpu.VMEM((nfreq, GRAM_ROWS, GRAM_ROWS), jnp.float32),
                pltpu.VMEM((nfreq, QUAD // 2, 128), jnp.bfloat16),
                pltpu.VMEM((n, QUAD // 2, 128), jnp.bfloat16),
                pltpu.VMEM((ns, QUAD // 2, 128), jnp.float32),
                dma((nchunk, n)),
                dma((nchunk, n)),
                dma((nchunk, n)),
                dma((nchunk, n)),
                dma((n,)),
                dma((n,)),
                dma((ns,)),
                dma((ns,)),
                dma((2, nchunk)),
            ]
            + [pltpu.VMEM((nt, width), jnp.bfloat16)] * nchunk,
            compiler_params=pltpu.CompilerParams(
                collective_id=0, has_side_effects=True, vmem_limit_bytes=60 * 1024 * 1024
            ),
            cost_estimate=cost,
        )(starts, freqs, alpha, series)
        own = spec.reshape(2, OWN_ROWS // 2, slab_cells)[:, :NBLK]
        return own[None], gram

    placed = (P("freq", "space"), P(), P(), P())
    return jax.shard_map(
        per_device,
        mesh=mesh,
        in_specs=placed,
        out_specs=(P("freq", None, None, "space"), P("freq", None, None, None)),
        check_vma=False,
    )
```

```python
import functools
import math

import jax
import jax.numpy as jnp
from jax import lax
from jax.experimental import pallas as pl
from jax.experimental.pallas import tpu as pltpu
from jax.sharding import PartitionSpec as P

NFFT = 512
NBLK = 7
HALF = 4
SHIFTS = 9
ORDER = SHIFTS * NBLK
QUAD = 64
GRAM_ROWS = 2 * QUAD
OWN_ROWS = 16
FREQ_ROWS = GRAM_ROWS + OWN_ROWS
GROUP = 4
MESH = pl.DeviceIdType.MESH


def half_turn_sine(steps):
    x = steps.astype(jnp.float32) * (math.pi / 256.0)
    x2 = x * x
    p = -1.0 / math.factorial(11)
    for order in (9, 7, 5, 3, 1):
        p = p * x2 + (-1.0) ** ((order - 1) // 2) / math.factorial(order)
    return p * x


def negative_cosine(step):
    folded = 128 - jnp.abs((step & (NFFT - 1)) - NFFT // 2)
    return half_turn_sine(folded)


def row_fields(starts):
    row = lax.broadcasted_iota(jnp.int32, (FREQ_ROWS, 128), 0)
    own = row >= GRAM_ROWS
    half = jnp.where(own, GRAM_ROWS + OWN_ROWS // 2, QUAD)
    part = jnp.where(row >= half, 1, 0)
    inner = jnp.where(own, row - GRAM_ROWS - OWN_ROWS // 2 * part, row - QUAD * part)
    shift = jnp.zeros_like(row)
    for bound in range(1, SHIFTS + 1):
        shift += jnp.where(inner >= NBLK * bound, 1, 0)
    block = jnp.where(own, inner, inner - NBLK * shift)
    used = inner < jnp.where(own, NBLK, ORDER)
    shift = jnp.where(own, HALF, shift)
    first = jnp.zeros_like(row)
    for index in range(NBLK):
        first = jnp.where(block == index, starts[index], first)
    return shift, part, first, used


def kernel(
    n,
    ns,
    nfreq,
    nchunk,
    total_cells,
    starts_ref,
    freqs_ref,
    alpha_ref,
    series_ref,
    spec_ref,
    gram_ref,
    table,
    weight,
    elapsed,
    stage,
    accum,
    pack_out,
    pack_in,
    space_parts,
    raw_send,
    raw_recv,
    spec_send,
    spec_recv,
    gram_send,
    gram_recv,
    space_send,
    space_recv,
    local_sem,
    *slabs,
):
    me = lax.axis_index("freq")
    my_space = lax.axis_index("space")
    rows, slab_cells = series_ref.shape
    nt = rows * n
    own_cells = slab_cells // n
    width = own_cells // nchunk

    def at_freq(peer):
        return {"freq": peer, "space": my_space}

    def at_space(peer):
        return {"freq": me, "space": peer}

    barrier = pltpu.get_barrier_semaphore()

    @pl.loop(1, n)
    def _(k):
        pl.semaphore_signal(
            barrier, inc=1, device_id=at_freq(lax.rem(me + k, n)), device_id_type=MESH
        )

    @pl.loop(1, ns)
    def _(k):
        pl.semaphore_signal(
            barrier, inc=1, device_id=at_space(lax.rem(my_space + k, ns)), device_id_type=MESH
        )

    pl.semaphore_wait(barrier, n + ns - 2)

    def raw_copy(c, peer, slot):
        cells = pl.ds(pl.multiple_of(peer * own_cells + c * width, 128), width)
        mine = pl.ds(pl.multiple_of(me * rows, rows), rows)
        return pltpu.make_async_remote_copy(
            src_ref=series_ref.at[:, cells],
            dst_ref=slabs[c].at[mine, :],
            send_sem=raw_send.at[c, peer],
            recv_sem=raw_recv.at[c, slot],
            device_id=at_freq(peer),
            device_id_type=MESH,
        )

    def own_copy(c):
        cells = pl.ds(pl.multiple_of(me * own_cells + c * width, 128), width)
        mine = pl.ds(pl.multiple_of(me * rows, rows), rows)
        return pltpu.make_async_copy(
            series_ref.at[:, cells], slabs[c].at[mine, :], local_sem.at[0, c]
        )

    def spec_copy(c, peer, slot):
        cells = pl.ds(pl.multiple_of(me * own_cells + c * width, 128), width)
        return pltpu.make_async_remote_copy(
            src_ref=stage.at[c, peer],
            dst_ref=spec_ref.at[:, cells],
            send_sem=spec_send.at[c, peer],
            recv_sem=spec_recv.at[c, slot],
            device_id=at_freq(peer),
            device_id_type=MESH,
        )

    def own_spec_copy(c):
        cells = pl.ds(pl.multiple_of(me * own_cells + c * width, 128), width)
        return pltpu.make_async_copy(
            stage.at[c, me], spec_ref.at[:, cells], local_sem.at[1, c]
        )

    def gram_copy(peer, slot):
        return pltpu.make_async_remote_copy(
            src_ref=pack_out.at[peer],
            dst_ref=pack_in.at[me],
            send_sem=gram_send.at[peer],
            recv_sem=gram_recv.at[slot],
            device_id=at_freq(peer),
            device_id_type=MESH,
        )

    def space_copy(peer, slot):
        return pltpu.make_async_remote_copy(
            src_ref=space_parts.at[my_space],
            dst_ref=space_parts.at[my_space],
            send_sem=space_send.at[peer],
            recv_sem=space_recv.at[slot],
            device_id=at_space(peer),
            device_id_type=MESH,
        )

    for c in range(nchunk):

        @pl.loop(0, n - 1)
        def _(k):
            away = 1 + lax.rem(k + n // 2 - 1, n - 1)
            raw_copy(c, lax.rem(me + away, n), me).start()

        own_copy(c).start()

    groups = nfreq // GROUP
    prow = lax.broadcasted_iota(jnp.int32, (QUAD, 128), 0)
    pcol = lax.broadcasted_iota(jnp.int32, (QUAD, 128), 1)
    left = lax.broadcasted_iota(jnp.int32, (QUAD // 2, 128), 1) < QUAD

    def packed(whole):
        turned = pltpu.roll(whole, QUAD, 1)
        real = whole[:QUAD] + turned[QUAD:]
        imag = turned[:QUAD] - whole[QUAD:]
        mixed = jnp.where(prow <= pcol, real, imag)
        low = pltpu.roll(mixed[QUAD // 2 :], QUAD, 1)
        return jnp.where(left, mixed[: QUAD // 2], low).astype(jnp.bfloat16)

    shift, part, first, used = row_fields([starts_ref[b] for b in range(NBLK)])
    quarter = part * (NFFT // 4)
    scale = 0.5 / math.sqrt(0.375 * NFFT)
    lane = lax.broadcasted_iota(jnp.int32, (FREQ_ROWS, 128), 1)

    @pl.loop(0, nt // 128)
    def _(i):
        cols = pl.ds(pl.multiple_of(i * 128, 128), 128)
        t = lane + i * 128 - first
        inside = (t >= 0) & (t < NFFT) & used
        window = scale + scale * negative_cosine(t)
        elapsed[:, cols] = t
        weight[:, cols] = jnp.where(inside, -window, 0.0)

    @pl.loop(0, nfreq)
    def _(j):
        bins = freqs_ref[j] + (shift - HALF) * alpha_ref[0]
        base = pl.multiple_of(j * FREQ_ROWS, 16)

        @pl.loop(0, nt // 128)
        def _(i):
            cols = pl.ds(pl.multiple_of(i * 128, 128), 128)
            step = bins * elapsed[:, cols] + quarter
            value = negative_cosine(step) * weight[:, cols]
            table[pl.ds(base, FREQ_ROWS), cols] = value.astype(jnp.bfloat16)

    for c in range(nchunk):
        own_copy(c).wait()

        @pl.loop(1, n)
        def _(k):
            peer = lax.rem(me + k, n)
            raw_copy(c, peer, peer).wait_recv()

        last = c == nchunk - 1

        @pl.loop(0, groups)
        def _(step):
            g = lax.rem(step + lax.div(me, GROUP) + groups // 2, groups)
            base = pl.multiple_of(g * (GROUP * FREQ_ROWS), 16)
            result = jnp.dot(
                table[pl.ds(base, GROUP * FREQ_ROWS), :],
                slabs[c][...],
                preferred_element_type=jnp.float32,
            ).astype(jnp.bfloat16)
            for i in range(GROUP):
                j = g * GROUP + i
                lines = result[i * FREQ_ROWS : i * FREQ_ROWS + GRAM_ROWS]
                stage[c, j] = result[i * FREQ_ROWS + GRAM_ROWS : (i + 1) * FREQ_ROWS]
                product = lax.dot_general(
                    lines, lines, (((1,), (1,)), ((), ())), preferred_element_type=jnp.float32
                )
                if c > 0:
                    product += accum[j]
                if last:
                    pack_out[j] = packed(product)
                else:
                    accum[j] = product
            for i in range(GROUP):
                j = g * GROUP + i

                @pl.when(j != me)
                def _():
                    if last:
                        gram_copy(j, me).start()
                    spec_copy(c, j, me).start()

        own_spec_copy(c).start()

    pack_in[me] = pack_out[me]

    @pl.loop(1, n)
    def _(k):
        peer = lax.rem(me + k, n)
        gram_copy(peer, peer).wait_recv()

    total = pack_in[0].astype(jnp.float32)
    for p in range(1, n):
        total += pack_in[p].astype(jnp.float32)
    space_parts[my_space] = total

    @pl.loop(1, ns)
    def _(k):
        space_copy(lax.rem(my_space + k, ns), my_space).start()

    @pl.loop(1, ns)
    def _(k):
        peer = lax.rem(my_space + k, ns)
        pltpu.make_async_remote_copy(
            src_ref=space_parts.at[my_space],
            dst_ref=space_parts.at[peer],
            send_sem=space_send.at[peer],
            recv_sem=space_recv.at[peer],
            device_id=at_space(peer),
            device_id_type=MESH,
        ).wait_recv()

    total = space_parts[0]
    for p in range(1, ns):
        total += space_parts[p]
    total = total * (1.0 / total_cells)
    mixed = jnp.concatenate(
        [total, pltpu.roll(total, QUAD, 1), jnp.zeros((QUAD, 128), jnp.float32)], axis=0
    )
    flipped = mixed.T[:QUAD]
    mixed = mixed[:QUAD]
    real = jnp.where(prow <= pcol, mixed, flipped)
    imag = jnp.where(prow > pcol, mixed, jnp.where(prow == pcol, 0.0, -flipped))
    gram_ref[0, 0] = real[:ORDER, :ORDER]
    gram_ref[0, 1] = imag[:ORDER, :ORDER]

    for c in range(nchunk):
        own_spec_copy(c).wait()

        @pl.loop(1, n)
        def _(k):
            peer = lax.rem(me + k, n)
            spec_copy(c, peer, peer).wait_recv()

    for c in range(nchunk):

        @pl.loop(1, n)
        def _(k):
            peer = lax.rem(me + k, n)
            raw_copy(c, peer, me).wait_send()
            spec_copy(c, peer, me).wait_send()

    @pl.loop(1, n)
    def _(k):
        peer = lax.rem(me + k, n)
        gram_copy(peer, me).wait_send()

    @pl.loop(1, ns)
    def _(k):
        space_copy(lax.rem(my_space + k, ns), my_space).wait_send()


def solution(mesh):
    n = mesh.shape["freq"]
    ns = mesh.shape["space"]

    def per_device(series, starts, freqs, alpha):
        rows, slab_cells = series.shape
        nfreq = freqs.shape[0]
        nt = rows * n
        own_cells = slab_cells // n
        nchunk = max(2, own_cells // 256)
        width = own_cells // nchunk
        smem = pl.BlockSpec(memory_space=pltpu.SMEM)
        table_rows = nfreq * FREQ_ROWS
        cost = pl.CostEstimate(
            flops=2 * table_rows * nt * own_cells,
            bytes_accessed=2 * rows * slab_cells * 2,
            transcendentals=0,
        )
        dma = pltpu.SemaphoreType.DMA
        spec, gram = pl.pallas_call(
            functools.partial(kernel, n, ns, nfreq, nchunk, slab_cells * ns),
            out_shape=(
                jax.ShapeDtypeStruct((OWN_ROWS, slab_cells), jnp.bfloat16),
                jax.ShapeDtypeStruct((1, 2, ORDER, ORDER), jnp.float32),
            ),
            in_specs=[smem, smem, smem, pl.BlockSpec(memory_space=pl.ANY)],
            out_specs=(
                pl.BlockSpec(memory_space=pl.ANY),
                pl.BlockSpec(memory_space=pltpu.VMEM),
            ),
            scratch_shapes=[
                pltpu.VMEM((table_rows, nt), jnp.bfloat16),
                pltpu.VMEM((FREQ_ROWS, nt), jnp.float32),
                pltpu.VMEM((FREQ_ROWS, nt), jnp.int32),
                pltpu.VMEM((nchunk, nfreq, OWN_ROWS, width), jnp.bfloat16),
                pltpu.VMEM((nfreq, GRAM_ROWS, GRAM_ROWS), jnp.float32),
                pltpu.VMEM((nfreq, QUAD // 2, 128), jnp.bfloat16),
                pltpu.VMEM((n, QUAD // 2, 128), jnp.bfloat16),
                pltpu.VMEM((ns, QUAD // 2, 128), jnp.float32),
                dma((nchunk, n)),
                dma((nchunk, n)),
                dma((nchunk, n)),
                dma((nchunk, n)),
                dma((n,)),
                dma((n,)),
                dma((ns,)),
                dma((ns,)),
                dma((2, nchunk)),
            ]
            + [pltpu.VMEM((nt, width), jnp.bfloat16)] * nchunk,
            compiler_params=pltpu.CompilerParams(
                collective_id=0, has_side_effects=True, vmem_limit_bytes=60 * 1024 * 1024
            ),
            cost_estimate=cost,
        )(starts, freqs, alpha, series)
        own = spec.reshape(2, OWN_ROWS // 2, slab_cells)[:, :NBLK]
        return own[None], gram

    placed = (P("freq", "space"), P(), P(), P())
    return jax.shard_map(
        per_device,
        mesh=mesh,
        in_specs=placed,
        out_specs=(P("freq", None, None, "space"), P("freq", None, None, None)),
        check_vma=False,
    )
```

```python
import functools
import math

import jax
import jax.numpy as jnp
from jax import lax
from jax.experimental import pallas as pl
from jax.experimental.pallas import tpu as pltpu
from jax.sharding import PartitionSpec as P

NFFT = 512
NBLK = 7
HALF = 4
SHIFTS = 9
ORDER = SHIFTS * NBLK
QUAD = 64
GRAM_ROWS = 2 * QUAD
OWN_ROWS = 16
FREQ_ROWS = GRAM_ROWS + OWN_ROWS
GROUP = 4
AHEAD = 2
MESH = pl.DeviceIdType.MESH


def half_turn_sine(steps):
    x = steps.astype(jnp.float32) * (math.pi / 256.0)
    x2 = x * x
    p = -1.0 / math.factorial(11)
    for order in (9, 7, 5, 3, 1):
        p = p * x2 + (-1.0) ** ((order - 1) // 2) / math.factorial(order)
    return p * x


def negative_cosine(step):
    folded = 128 - jnp.abs((step & (NFFT - 1)) - NFFT // 2)
    return half_turn_sine(folded)


def row_fields(starts):
    row = lax.broadcasted_iota(jnp.int32, (FREQ_ROWS, 128), 0)
    own = row >= GRAM_ROWS
    half = jnp.where(own, GRAM_ROWS + OWN_ROWS // 2, QUAD)
    part = jnp.where(row >= half, 1, 0)
    inner = jnp.where(own, row - GRAM_ROWS - OWN_ROWS // 2 * part, row - QUAD * part)
    shift = jnp.zeros_like(row)
    for bound in range(1, SHIFTS + 1):
        shift += jnp.where(inner >= NBLK * bound, 1, 0)
    block = jnp.where(own, inner, inner - NBLK * shift)
    used = inner < jnp.where(own, NBLK, ORDER)
    shift = jnp.where(own, HALF, shift)
    first = jnp.zeros_like(row)
    for index in range(NBLK):
        first = jnp.where(block == index, starts[index], first)
    return shift, part, first, used


def kernel(
    n,
    ns,
    nfreq,
    nchunk,
    total_cells,
    starts_ref,
    freqs_ref,
    alpha_ref,
    series_ref,
    spec_ref,
    gram_ref,
    table,
    weight,
    elapsed,
    stage,
    accum,
    pack_out,
    pack_in,
    space_parts,
    raw_send,
    raw_recv,
    spec_send,
    spec_recv,
    gram_send,
    gram_recv,
    space_send,
    space_recv,
    local_sem,
    *slabs,
):
    me = lax.axis_index("freq")
    my_space = lax.axis_index("space")
    rows, slab_cells = series_ref.shape
    nt = rows * n
    own_cells = slab_cells // n
    width = own_cells // nchunk

    def at_freq(peer):
        return {"freq": peer, "space": my_space}

    def at_space(peer):
        return {"freq": me, "space": peer}

    barrier = pltpu.get_barrier_semaphore()

    @pl.loop(1, n)
    def _(k):
        pl.semaphore_signal(
            barrier, inc=1, device_id=at_freq(lax.rem(me + k, n)), device_id_type=MESH
        )

    @pl.loop(1, ns)
    def _(k):
        pl.semaphore_signal(
            barrier, inc=1, device_id=at_space(lax.rem(my_space + k, ns)), device_id_type=MESH
        )

    pl.semaphore_wait(barrier, n + ns - 2)

    def raw_copy(c, peer, slot):
        cells = pl.ds(pl.multiple_of(peer * own_cells + c * width, 128), width)
        mine = pl.ds(pl.multiple_of(me * rows, rows), rows)
        return pltpu.make_async_remote_copy(
            src_ref=series_ref.at[:, cells],
            dst_ref=slabs[c].at[mine, :],
            send_sem=raw_send.at[c, peer],
            recv_sem=raw_recv.at[c, slot],
            device_id=at_freq(peer),
            device_id_type=MESH,
        )

    def own_copy(c):
        cells = pl.ds(pl.multiple_of(me * own_cells + c * width, 128), width)
        mine = pl.ds(pl.multiple_of(me * rows, rows), rows)
        return pltpu.make_async_copy(
            series_ref.at[:, cells], slabs[c].at[mine, :], local_sem.at[0, c]
        )

    def spec_copy(c, peer, slot):
        cells = pl.ds(pl.multiple_of(me * own_cells + c * width, 128), width)
        return pltpu.make_async_remote_copy(
            src_ref=stage.at[c, peer],
            dst_ref=spec_ref.at[:, cells],
            send_sem=spec_send.at[c, peer],
            recv_sem=spec_recv.at[c, slot],
            device_id=at_freq(peer),
            device_id_type=MESH,
        )

    def own_spec_copy(c):
        cells = pl.ds(pl.multiple_of(me * own_cells + c * width, 128), width)
        return pltpu.make_async_copy(
            stage.at[c, me], spec_ref.at[:, cells], local_sem.at[1, c]
        )

    def gram_copy(peer, slot):
        return pltpu.make_async_remote_copy(
            src_ref=pack_out.at[peer],
            dst_ref=pack_in.at[me],
            send_sem=gram_send.at[peer],
            recv_sem=gram_recv.at[slot],
            device_id=at_freq(peer),
            device_id_type=MESH,
        )

    def space_copy(peer, slot):
        return pltpu.make_async_remote_copy(
            src_ref=space_parts.at[my_space],
            dst_ref=space_parts.at[my_space],
            send_sem=space_send.at[peer],
            recv_sem=space_recv.at[slot],
            device_id=at_space(peer),
            device_id_type=MESH,
        )

    def start_chunk(c):
        @pl.loop(0, n - 1)
        def _(k):
            away = 1 + lax.rem(k + n // 2 - 1, n - 1)
            raw_copy(c, lax.rem(me + away, n), me).start()

        own_copy(c).start()

    for c in range(AHEAD):
        start_chunk(c)

    groups = nfreq // GROUP
    prow = lax.broadcasted_iota(jnp.int32, (QUAD, 128), 0)
    pcol = lax.broadcasted_iota(jnp.int32, (QUAD, 128), 1)
    left = lax.broadcasted_iota(jnp.int32, (QUAD // 2, 128), 1) < QUAD

    def packed(whole):
        turned = pltpu.roll(whole, QUAD, 1)
        real = whole[:QUAD] + turned[QUAD:]
        imag = turned[:QUAD] - whole[QUAD:]
        mixed = jnp.where(prow <= pcol, real, imag)
        low = pltpu.roll(mixed[QUAD // 2 :], QUAD, 1)
        return jnp.where(left, mixed[: QUAD // 2], low).astype(jnp.bfloat16)

    shift, part, first, used = row_fields([starts_ref[b] for b in range(NBLK)])
    quarter = part * (NFFT // 4)
    scale = 0.5 / math.sqrt(0.375 * NFFT)
    lane = lax.broadcasted_iota(jnp.int32, (FREQ_ROWS, 128), 1)

    @pl.loop(0, nt // 128)
    def _(i):
        cols = pl.ds(pl.multiple_of(i * 128, 128), 128)
        t = lane + i * 128 - first
        inside = (t >= 0) & (t < NFFT) & used
        window = scale + scale * negative_cosine(t)
        elapsed[:, cols] = t
        weight[:, cols] = jnp.where(inside, -window, 0.0)

    @pl.loop(0, nfreq)
    def _(j):
        bins = freqs_ref[j] + (shift - HALF) * alpha_ref[0]
        base = pl.multiple_of(j * FREQ_ROWS, 16)

        @pl.loop(0, nt // 128)
        def _(i):
            cols = pl.ds(pl.multiple_of(i * 128, 128), 128)
            step = bins * elapsed[:, cols] + quarter
            value = negative_cosine(step) * weight[:, cols]
            table[pl.ds(base, FREQ_ROWS), cols] = value.astype(jnp.bfloat16)

    for c in range(nchunk):
        own_copy(c).wait()

        @pl.loop(1, n)
        def _(k):
            peer = lax.rem(me + k, n)
            raw_copy(c, peer, peer).wait_recv()

        @pl.loop(1, n)
        def _(k):
            raw_copy(c, lax.rem(me + k, n), me).wait_send()

        if c + AHEAD < nchunk:
            start_chunk(c + AHEAD)

        last = c == nchunk - 1

        @pl.loop(0, groups)
        def _(step):
            g = lax.rem(step + lax.div(me, GROUP) + groups // 2, groups)
            base = pl.multiple_of(g * (GROUP * FREQ_ROWS), 16)
            result = jnp.dot(
                table[pl.ds(base, GROUP * FREQ_ROWS), :],
                slabs[c][...],
                preferred_element_type=jnp.float32,
            ).astype(jnp.bfloat16)
            for i in range(GROUP):
                j = g * GROUP + i
                lines = result[i * FREQ_ROWS : i * FREQ_ROWS + GRAM_ROWS]
                stage[c, j] = result[i * FREQ_ROWS + GRAM_ROWS : (i + 1) * FREQ_ROWS]
                product = lax.dot_general(
                    lines, lines, (((1,), (1,)), ((), ())), preferred_element_type=jnp.float32
                )
                if c > 0:
                    product += accum[j]
                if last:
                    pack_out[j] = packed(product)
                else:
                    accum[j] = product
            for i in range(GROUP):
                j = g * GROUP + i

                @pl.when(j != me)
                def _():
                    if last:
                        gram_copy(j, me).start()
                    spec_copy(c, j, me).start()

        own_spec_copy(c).start()

    pack_in[me] = pack_out[me]

    @pl.loop(1, n)
    def _(k):
        peer = lax.rem(me + k, n)
        gram_copy(peer, peer).wait_recv()

    total = pack_in[0].astype(jnp.float32)
    for p in range(1, n):
        total += pack_in[p].astype(jnp.float32)
    space_parts[my_space] = total

    @pl.loop(1, ns)
    def _(k):
        space_copy(lax.rem(my_space + k, ns), my_space).start()

    @pl.loop(1, ns)
    def _(k):
        peer = lax.rem(my_space + k, ns)
        pltpu.make_async_remote_copy(
            src_ref=space_parts.at[my_space],
            dst_ref=space_parts.at[peer],
            send_sem=space_send.at[peer],
            recv_sem=space_recv.at[peer],
            device_id=at_space(peer),
            device_id_type=MESH,
        ).wait_recv()

    total = space_parts[0]
    for p in range(1, ns):
        total += space_parts[p]
    total = total * (1.0 / total_cells)
    mixed = jnp.concatenate(
        [total, pltpu.roll(total, QUAD, 1), jnp.zeros((QUAD, 128), jnp.float32)], axis=0
    )
    flipped = mixed.T[:QUAD]
    mixed = mixed[:QUAD]
    real = jnp.where(prow <= pcol, mixed, flipped)
    imag = jnp.where(prow > pcol, mixed, jnp.where(prow == pcol, 0.0, -flipped))
    gram_ref[0, 0] = real[:ORDER, :ORDER]
    gram_ref[0, 1] = imag[:ORDER, :ORDER]

    for c in range(nchunk):
        own_spec_copy(c).wait()

        @pl.loop(1, n)
        def _(k):
            peer = lax.rem(me + k, n)
            spec_copy(c, peer, peer).wait_recv()

    for c in range(nchunk):

        @pl.loop(1, n)
        def _(k):
            peer = lax.rem(me + k, n)
            spec_copy(c, peer, me).wait_send()

    @pl.loop(1, n)
    def _(k):
        peer = lax.rem(me + k, n)
        gram_copy(peer, me).wait_send()

    @pl.loop(1, ns)
    def _(k):
        space_copy(lax.rem(my_space + k, ns), my_space).wait_send()


def solution(mesh):
    n = mesh.shape["freq"]
    ns = mesh.shape["space"]

    def per_device(series, starts, freqs, alpha):
        rows, slab_cells = series.shape
        nfreq = freqs.shape[0]
        nt = rows * n
        own_cells = slab_cells // n
        nchunk = max(2, own_cells // 256)
        width = own_cells // nchunk
        smem = pl.BlockSpec(memory_space=pltpu.SMEM)
        table_rows = nfreq * FREQ_ROWS
        cost = pl.CostEstimate(
            flops=2 * table_rows * nt * own_cells,
            bytes_accessed=2 * rows * slab_cells * 2,
            transcendentals=0,
        )
        dma = pltpu.SemaphoreType.DMA
        spec, gram = pl.pallas_call(
            functools.partial(kernel, n, ns, nfreq, nchunk, slab_cells * ns),
            out_shape=(
                jax.ShapeDtypeStruct((OWN_ROWS, slab_cells), jnp.bfloat16),
                jax.ShapeDtypeStruct((1, 2, ORDER, ORDER), jnp.float32),
            ),
            in_specs=[smem, smem, smem, pl.BlockSpec(memory_space=pl.ANY)],
            out_specs=(
                pl.BlockSpec(memory_space=pl.ANY),
                pl.BlockSpec(memory_space=pltpu.VMEM),
            ),
            scratch_shapes=[
                pltpu.VMEM((table_rows, nt), jnp.bfloat16),
                pltpu.VMEM((FREQ_ROWS, nt), jnp.float32),
                pltpu.VMEM((FREQ_ROWS, nt), jnp.int32),
                pltpu.VMEM((nchunk, nfreq, OWN_ROWS, width), jnp.bfloat16),
                pltpu.VMEM((nfreq, GRAM_ROWS, GRAM_ROWS), jnp.float32),
                pltpu.VMEM((nfreq, QUAD // 2, 128), jnp.bfloat16),
                pltpu.VMEM((n, QUAD // 2, 128), jnp.bfloat16),
                pltpu.VMEM((ns, QUAD // 2, 128), jnp.float32),
                dma((nchunk, n)),
                dma((nchunk, n)),
                dma((nchunk, n)),
                dma((nchunk, n)),
                dma((n,)),
                dma((n,)),
                dma((ns,)),
                dma((ns,)),
                dma((2, nchunk)),
            ]
            + [pltpu.VMEM((nt, width), jnp.bfloat16)] * nchunk,
            compiler_params=pltpu.CompilerParams(
                collective_id=0, has_side_effects=True, vmem_limit_bytes=60 * 1024 * 1024
            ),
            cost_estimate=cost,
        )(starts, freqs, alpha, series)
        own = spec.reshape(2, OWN_ROWS // 2, slab_cells)[:, :NBLK]
        return own[None], gram

    placed = (P("freq", "space"), P(), P(), P())
    return jax.shard_map(
        per_device,
        mesh=mesh,
        in_specs=placed,
        out_specs=(P("freq", None, None, "space"), P("freq", None, None, None)),
        check_vma=False,
    )
```

```python
import functools
import math

import jax
import jax.numpy as jnp
from jax import lax
from jax.experimental import pallas as pl
from jax.experimental.pallas import tpu as pltpu
from jax.sharding import PartitionSpec as P

NFFT = 512
NBLK = 7
HALF = 4
SHIFTS = 9
ORDER = SHIFTS * NBLK
QUAD = 64
GRAM_ROWS = 2 * QUAD
OWN_ROWS = 16
FREQ_ROWS = GRAM_ROWS + OWN_ROWS
GROUP = 4
MESH = pl.DeviceIdType.MESH


def half_turn_sine(steps):
    x = steps.astype(jnp.float32) * (math.pi / 256.0)
    x2 = x * x
    p = -1.0 / math.factorial(11)
    for order in (9, 7, 5, 3, 1):
        p = p * x2 + (-1.0) ** ((order - 1) // 2) / math.factorial(order)
    return p * x


def negative_cosine(step):
    folded = 128 - jnp.abs((step & (NFFT - 1)) - NFFT // 2)
    return half_turn_sine(folded)


def row_fields(starts):
    row = lax.broadcasted_iota(jnp.int32, (FREQ_ROWS, 128), 0)
    own = row >= GRAM_ROWS
    part = jnp.where(own, row & 1, jnp.where(row >= QUAD, 1, 0))
    inner = jnp.where(own, (row - GRAM_ROWS) >> 1, row - QUAD * part)
    shift = jnp.zeros_like(row)
    for bound in range(1, SHIFTS + 1):
        shift += jnp.where(inner >= NBLK * bound, 1, 0)
    block = jnp.where(own, inner, inner - NBLK * shift)
    used = inner < jnp.where(own, NBLK, ORDER)
    shift = jnp.where(own, HALF, shift)
    first = jnp.zeros_like(row)
    for index in range(NBLK):
        first = jnp.where(block == index, starts[index], first)
    return shift, part, first, used


def kernel(
    n,
    ns,
    nfreq,
    nchunk,
    total_cells,
    starts_ref,
    freqs_ref,
    alpha_ref,
    series_ref,
    spec_ref,
    gram_ref,
    table,
    weight,
    elapsed,
    stage,
    outgoing,
    accum,
    pack_out,
    pack_in,
    space_parts,
    raw_send,
    raw_recv,
    spec_send,
    spec_recv,
    gram_send,
    gram_recv,
    space_send,
    space_recv,
    local_sem,
    stage_sem,
    *slabs,
):
    me = lax.axis_index("freq")
    my_space = lax.axis_index("space")
    rows, slab_cells = series_ref.shape
    nt = rows * n
    own_cells = slab_cells // n
    width = own_cells // nchunk

    def at_freq(peer):
        return {"freq": peer, "space": my_space}

    def at_space(peer):
        return {"freq": me, "space": peer}

    def stage_copy(c, peer):
        cells = pl.ds(pl.multiple_of(peer * own_cells + c * width, 128), width)
        return pltpu.make_async_copy(
            series_ref.at[:, cells], outgoing.at[c, peer], stage_sem.at[c, peer]
        )

    def peer_at(k):
        return lax.rem(me + 1 + lax.rem(k + n // 2 - 1, n - 1), n)

    barrier = pltpu.get_barrier_semaphore()

    @pl.loop(1, n)
    def _(k):
        pl.semaphore_signal(
            barrier, inc=1, device_id=at_freq(lax.rem(me + k, n)), device_id_type=MESH
        )

    @pl.loop(1, ns)
    def _(k):
        pl.semaphore_signal(
            barrier, inc=1, device_id=at_space(lax.rem(my_space + k, ns)), device_id_type=MESH
        )

    for c in range(nchunk):

        @pl.loop(0, n - 1)
        def _(k):
            stage_copy(c, peer_at(k)).start()

    pl.semaphore_wait(barrier, n + ns - 2)

    def raw_copy(c, peer, slot):
        mine = pl.ds(pl.multiple_of(me * rows, rows), rows)
        return pltpu.make_async_remote_copy(
            src_ref=outgoing.at[c, peer],
            dst_ref=slabs[c].at[mine, :],
            send_sem=raw_send.at[c, peer],
            recv_sem=raw_recv.at[c, slot],
            device_id=at_freq(peer),
            device_id_type=MESH,
        )

    def own_copy(c):
        cells = pl.ds(pl.multiple_of(me * own_cells + c * width, 128), width)
        mine = pl.ds(pl.multiple_of(me * rows, rows), rows)
        return pltpu.make_async_copy(
            series_ref.at[:, cells], slabs[c].at[mine, :], local_sem.at[0, c]
        )

    def spec_copy(c, peer, slot):
        cells = pl.ds(pl.multiple_of(me * own_cells + c * width, 128), width)
        return pltpu.make_async_remote_copy(
            src_ref=stage.at[c, peer],
            dst_ref=spec_ref.at[:, :, cells],
            send_sem=spec_send.at[c, peer],
            recv_sem=spec_recv.at[c, slot],
            device_id=at_freq(peer),
            device_id_type=MESH,
        )

    def own_spec_copy(c):
        cells = pl.ds(pl.multiple_of(me * own_cells + c * width, 128), width)
        return pltpu.make_async_copy(
            stage.at[c, me], spec_ref.at[:, :, cells], local_sem.at[1, c]
        )

    def gram_copy(peer, slot):
        return pltpu.make_async_remote_copy(
            src_ref=pack_out.at[peer],
            dst_ref=pack_in.at[me],
            send_sem=gram_send.at[peer],
            recv_sem=gram_recv.at[slot],
            device_id=at_freq(peer),
            device_id_type=MESH,
        )

    def space_copy(peer, slot):
        return pltpu.make_async_remote_copy(
            src_ref=space_parts.at[my_space],
            dst_ref=space_parts.at[my_space],
            send_sem=space_send.at[peer],
            recv_sem=space_recv.at[slot],
            device_id=at_space(peer),
            device_id_type=MESH,
        )

    for c in range(nchunk):

        @pl.loop(0, n - 1)
        def _(k):
            peer = peer_at(k)
            stage_copy(c, peer).wait()
            raw_copy(c, peer, me).start()

        own_copy(c).start()

    groups = nfreq // GROUP
    prow = lax.broadcasted_iota(jnp.int32, (QUAD, 128), 0)
    pcol = lax.broadcasted_iota(jnp.int32, (QUAD, 128), 1)
    left = lax.broadcasted_iota(jnp.int32, (QUAD // 2, 128), 1) < QUAD

    def packed(whole):
        turned = pltpu.roll(whole, QUAD, 1)
        real = whole[:QUAD] + turned[QUAD:]
        imag = turned[:QUAD] - whole[QUAD:]
        mixed = jnp.where(prow <= pcol, real, imag)
        low = pltpu.roll(mixed[QUAD // 2 :], QUAD, 1)
        return jnp.where(left, mixed[: QUAD // 2], low).astype(jnp.bfloat16)

    shift, part, first, used = row_fields([starts_ref[b] for b in range(NBLK)])
    quarter = part * (NFFT // 4)
    scale = 0.5 / math.sqrt(0.375 * NFFT)
    lane = lax.broadcasted_iota(jnp.int32, (FREQ_ROWS, 128), 1)

    @pl.loop(0, nt // 128)
    def _(i):
        cols = pl.ds(pl.multiple_of(i * 128, 128), 128)
        t = lane + i * 128 - first
        inside = (t >= 0) & (t < NFFT) & used
        window = scale + scale * negative_cosine(t)
        elapsed[:, cols] = t
        weight[:, cols] = jnp.where(inside, -window, 0.0)

    @pl.loop(0, nfreq)
    def _(j):
        bins = freqs_ref[j] + (shift - HALF) * alpha_ref[0]
        base = pl.multiple_of(j * FREQ_ROWS, 16)

        @pl.loop(0, nt // 128)
        def _(i):
            cols = pl.ds(pl.multiple_of(i * 128, 128), 128)
            step = bins * elapsed[:, cols] + quarter
            value = negative_cosine(step) * weight[:, cols]
            table[pl.ds(base, FREQ_ROWS), cols] = value.astype(jnp.bfloat16)

    for c in range(nchunk):
        own_copy(c).wait()

        @pl.loop(1, n)
        def _(k):
            peer = lax.rem(me + k, n)
            raw_copy(c, peer, peer).wait_recv()

        last = c == nchunk - 1

        @pl.loop(0, groups)
        def _(step):
            g = lax.rem(step + lax.div(me, GROUP) + groups // 2, groups)
            base = pl.multiple_of(g * (GROUP * FREQ_ROWS), 16)
            result = jnp.dot(
                table[pl.ds(base, GROUP * FREQ_ROWS), :],
                slabs[c][...],
                preferred_element_type=jnp.float32,
            ).astype(jnp.bfloat16)
            for i in range(GROUP):
                j = g * GROUP + i
                lines = result[i * FREQ_ROWS : i * FREQ_ROWS + GRAM_ROWS]
                first = i * FREQ_ROWS + GRAM_ROWS
                stage[c, j] = result[first : first + 2 * NBLK].reshape(NBLK, 2, width)
                product = lax.dot_general(
                    lines, lines, (((1,), (1,)), ((), ())), preferred_element_type=jnp.float32
                )
                if c > 0:
                    product += accum[j]
                if last:
                    pack_out[j] = packed(product)
                else:
                    accum[j] = product
            for i in range(GROUP):
                j = g * GROUP + i

                @pl.when(j != me)
                def _():
                    if last:
                        gram_copy(j, me).start()
                    spec_copy(c, j, me).start()

        own_spec_copy(c).start()

    pack_in[me] = pack_out[me]

    @pl.loop(1, n)
    def _(k):
        peer = lax.rem(me + k, n)
        gram_copy(peer, peer).wait_recv()

    total = pack_in[0].astype(jnp.float32)
    for p in range(1, n):
        total += pack_in[p].astype(jnp.float32)
    space_parts[my_space] = total

    @pl.loop(1, ns)
    def _(k):
        space_copy(lax.rem(my_space + k, ns), my_space).start()

    @pl.loop(1, ns)
    def _(k):
        peer = lax.rem(my_space + k, ns)
        pltpu.make_async_remote_copy(
            src_ref=space_parts.at[my_space],
            dst_ref=space_parts.at[peer],
            send_sem=space_send.at[peer],
            recv_sem=space_recv.at[peer],
            device_id=at_space(peer),
            device_id_type=MESH,
        ).wait_recv()

    total = space_parts[0]
    for p in range(1, ns):
        total += space_parts[p]
    total = total * (1.0 / total_cells)
    mixed = jnp.concatenate(
        [total, pltpu.roll(total, QUAD, 1), jnp.zeros((QUAD, 128), jnp.float32)], axis=0
    )
    flipped = mixed.T[:QUAD]
    mixed = mixed[:QUAD]
    real = jnp.where(prow <= pcol, mixed, flipped)
    imag = jnp.where(prow > pcol, mixed, jnp.where(prow == pcol, 0.0, -flipped))
    gram_ref[0, :, 0] = real[:ORDER, :ORDER]
    gram_ref[0, :, 1] = imag[:ORDER, :ORDER]

    for c in range(nchunk):
        own_spec_copy(c).wait()

        @pl.loop(1, n)
        def _(k):
            peer = lax.rem(me + k, n)
            spec_copy(c, peer, peer).wait_recv()

    for c in range(nchunk):

        @pl.loop(1, n)
        def _(k):
            peer = lax.rem(me + k, n)
            raw_copy(c, peer, me).wait_send()
            spec_copy(c, peer, me).wait_send()

    @pl.loop(1, n)
    def _(k):
        peer = lax.rem(me + k, n)
        gram_copy(peer, me).wait_send()

    @pl.loop(1, ns)
    def _(k):
        space_copy(lax.rem(my_space + k, ns), my_space).wait_send()


def solution(mesh):
    n = mesh.shape["freq"]
    ns = mesh.shape["space"]

    def per_device(series, starts, freqs, alpha):
        rows, slab_cells = series.shape
        nfreq = freqs.shape[0]
        nt = rows * n
        own_cells = slab_cells // n
        nchunk = max(2, own_cells // 256)
        width = own_cells // nchunk
        smem = pl.BlockSpec(memory_space=pltpu.SMEM)
        table_rows = nfreq * FREQ_ROWS
        cost = pl.CostEstimate(
            flops=2 * table_rows * nt * own_cells,
            bytes_accessed=2 * rows * slab_cells * 2,
            transcendentals=0,
        )
        dma = pltpu.SemaphoreType.DMA
        spec, gram = pl.pallas_call(
            functools.partial(kernel, n, ns, nfreq, nchunk, slab_cells * ns),
            out_shape=(
                jax.ShapeDtypeStruct((NBLK, 2, slab_cells), jnp.bfloat16),
                jax.ShapeDtypeStruct((1, ORDER, 2, ORDER), jnp.float32),
            ),
            in_specs=[smem, smem, smem, pl.BlockSpec(memory_space=pl.ANY)],
            out_specs=(
                pl.BlockSpec(memory_space=pl.ANY),
                pl.BlockSpec(memory_space=pltpu.VMEM),
            ),
            scratch_shapes=[
                pltpu.VMEM((table_rows, nt), jnp.bfloat16),
                pltpu.VMEM((FREQ_ROWS, nt), jnp.float32),
                pltpu.VMEM((FREQ_ROWS, nt), jnp.int32),
                pltpu.VMEM((nchunk, nfreq, NBLK, 2, width), jnp.bfloat16),
                pltpu.VMEM((nchunk, n, rows, width), jnp.bfloat16),
                pltpu.VMEM((nfreq, GRAM_ROWS, GRAM_ROWS), jnp.float32),
                pltpu.VMEM((nfreq, QUAD // 2, 128), jnp.bfloat16),
                pltpu.VMEM((n, QUAD // 2, 128), jnp.bfloat16),
                pltpu.VMEM((ns, QUAD // 2, 128), jnp.float32),
                dma((nchunk, n)),
                dma((nchunk, n)),
                dma((nchunk, n)),
                dma((nchunk, n)),
                dma((n,)),
                dma((n,)),
                dma((ns,)),
                dma((ns,)),
                dma((2, nchunk)),
                dma((nchunk, n)),
            ]
            + [pltpu.VMEM((nt, width), jnp.bfloat16)] * nchunk,
            compiler_params=pltpu.CompilerParams(
                collective_id=0, has_side_effects=True, vmem_limit_bytes=60 * 1024 * 1024
            ),
            cost_estimate=cost,
        )(starts, freqs, alpha, series)
        own = jnp.transpose(spec, (1, 0, 2))
        return own[None], jnp.transpose(gram, (0, 2, 1, 3))

    placed = (P("freq", "space"), P(), P(), P())
    return jax.shard_map(
        per_device,
        mesh=mesh,
        in_specs=placed,
        out_specs=(P("freq", None, None, "space"), P("freq", None, None, None)),
        check_vma=False,
    )
```

```python
import functools
import math

import jax
import jax.numpy as jnp
from jax import lax
from jax.experimental import pallas as pl
from jax.experimental.pallas import tpu as pltpu
from jax.sharding import PartitionSpec as P

NFFT = 512
NBLK = 7
HALF = 4
SHIFTS = 9
ORDER = SHIFTS * NBLK
QUAD = 64
GRAM_ROWS = 2 * QUAD
OWN_ROWS = 16
FREQ_ROWS = GRAM_ROWS + OWN_ROWS
GROUP = 4
MESH = pl.DeviceIdType.MESH


def half_turn_sine(steps):
    x = steps.astype(jnp.float32) * (math.pi / 256.0)
    x2 = x * x
    p = -1.0 / math.factorial(11)
    for order in (9, 7, 5, 3, 1):
        p = p * x2 + (-1.0) ** ((order - 1) // 2) / math.factorial(order)
    return p * x


def negative_cosine(step):
    folded = 128 - jnp.abs((step & (NFFT - 1)) - NFFT // 2)
    return half_turn_sine(folded)


def row_fields(starts):
    row = lax.broadcasted_iota(jnp.int32, (FREQ_ROWS, 128), 0)
    own = row >= GRAM_ROWS
    part = jnp.where(own, row & 1, jnp.where(row >= QUAD, 1, 0))
    inner = jnp.where(own, (row - GRAM_ROWS) >> 1, row - QUAD * part)
    shift = jnp.zeros_like(row)
    for bound in range(1, SHIFTS + 1):
        shift += jnp.where(inner >= NBLK * bound, 1, 0)
    block = jnp.where(own, inner, inner - NBLK * shift)
    used = inner < jnp.where(own, NBLK, ORDER)
    shift = jnp.where(own, HALF, shift)
    first = jnp.zeros_like(row)
    for index in range(NBLK):
        first = jnp.where(block == index, starts[index], first)
    return shift, part, first, used


def kernel(
    n,
    ns,
    nfreq,
    nchunk,
    total_cells,
    starts_ref,
    freqs_ref,
    alpha_ref,
    series_ref,
    spec_ref,
    gram_ref,
    table,
    weight,
    stage,
    outgoing,
    accum,
    pack_out,
    pack_in,
    space_parts,
    raw_send,
    raw_recv,
    spec_send,
    spec_recv,
    gram_send,
    gram_recv,
    space_send,
    space_recv,
    local_sem,
    stage_sem,
    *slabs,
):
    me = lax.axis_index("freq")
    my_space = lax.axis_index("space")
    rows, slab_cells = series_ref.shape
    nt = rows * n
    own_cells = slab_cells // n
    width = own_cells // nchunk

    def at_freq(peer):
        return {"freq": peer, "space": my_space}

    def at_space(peer):
        return {"freq": me, "space": peer}

    def stage_copy(c, peer):
        cells = pl.ds(pl.multiple_of(peer * own_cells + c * width, 128), width)
        return pltpu.make_async_copy(
            series_ref.at[:, cells], outgoing.at[c, peer], stage_sem.at[c, peer]
        )

    def peer_at(k):
        return lax.rem(me + 1 + lax.rem(k + n // 2 - 1, n - 1), n)

    barrier = pltpu.get_barrier_semaphore()

    @pl.loop(1, n)
    def _(k):
        pl.semaphore_signal(
            barrier, inc=1, device_id=at_freq(lax.rem(me + k, n)), device_id_type=MESH
        )

    @pl.loop(1, ns)
    def _(k):
        pl.semaphore_signal(
            barrier, inc=1, device_id=at_space(lax.rem(my_space + k, ns)), device_id_type=MESH
        )

    for c in range(nchunk):

        @pl.loop(0, n - 1)
        def _(k):
            stage_copy(c, peer_at(k)).start()

    pl.semaphore_wait(barrier, n + ns - 2)

    def raw_copy(c, peer, slot):
        mine = pl.ds(pl.multiple_of(me * rows, rows), rows)
        return pltpu.make_async_remote_copy(
            src_ref=outgoing.at[c, peer],
            dst_ref=slabs[c].at[mine, :],
            send_sem=raw_send.at[c, peer],
            recv_sem=raw_recv.at[c, slot],
            device_id=at_freq(peer),
            device_id_type=MESH,
        )

    def own_copy(c):
        cells = pl.ds(pl.multiple_of(me * own_cells + c * width, 128), width)
        mine = pl.ds(pl.multiple_of(me * rows, rows), rows)
        return pltpu.make_async_copy(
            series_ref.at[:, cells], slabs[c].at[mine, :], local_sem.at[0, c]
        )

    def spec_copy(c, peer, slot):
        cells = pl.ds(pl.multiple_of(me * own_cells + c * width, 128), width)
        return pltpu.make_async_remote_copy(
            src_ref=stage.at[c, peer],
            dst_ref=spec_ref.at[:, :, cells],
            send_sem=spec_send.at[c, peer],
            recv_sem=spec_recv.at[c, slot],
            device_id=at_freq(peer),
            device_id_type=MESH,
        )

    def own_spec_copy(c):
        cells = pl.ds(pl.multiple_of(me * own_cells + c * width, 128), width)
        return pltpu.make_async_copy(
            stage.at[c, me], spec_ref.at[:, :, cells], local_sem.at[1, c]
        )

    def gram_copy(peer, slot):
        return pltpu.make_async_remote_copy(
            src_ref=pack_out.at[peer],
            dst_ref=pack_in.at[me],
            send_sem=gram_send.at[peer],
            recv_sem=gram_recv.at[slot],
            device_id=at_freq(peer),
            device_id_type=MESH,
        )

    def space_copy(peer, slot):
        return pltpu.make_async_remote_copy(
            src_ref=space_parts.at[my_space],
            dst_ref=space_parts.at[my_space],
            send_sem=space_send.at[peer],
            recv_sem=space_recv.at[slot],
            device_id=at_space(peer),
            device_id_type=MESH,
        )

    for c in range(nchunk):

        @pl.loop(0, n - 1)
        def _(k):
            peer = peer_at(k)
            stage_copy(c, peer).wait()
            raw_copy(c, peer, me).start()

        own_copy(c).start()

    groups = nfreq // GROUP
    prow = lax.broadcasted_iota(jnp.int32, (QUAD, 128), 0)
    pcol = lax.broadcasted_iota(jnp.int32, (QUAD, 128), 1)
    left = lax.broadcasted_iota(jnp.int32, (QUAD // 2, 128), 1) < QUAD

    def packed(whole):
        turned = pltpu.roll(whole, QUAD, 1)
        real = whole[:QUAD] + turned[QUAD:]
        imag = turned[:QUAD] - whole[QUAD:]
        mixed = jnp.where(prow <= pcol, real, imag)
        low = pltpu.roll(mixed[QUAD // 2 :], QUAD, 1)
        return jnp.where(left, mixed[: QUAD // 2], low).astype(jnp.bfloat16)

    shift, part, first, used = row_fields([starts_ref[b] for b in range(NBLK)])
    quarter = part * (NFFT // 4)
    scale = 0.5 / math.sqrt(0.375 * NFFT)
    lane = lax.broadcasted_iota(jnp.int32, (FREQ_ROWS, 128), 1)

    @pl.loop(0, nt // 128)
    def _(i):
        cols = pl.ds(pl.multiple_of(i * 128, 128), 128)
        t = lane + i * 128 - first
        inside = (t >= 0) & (t < NFFT) & used
        window = scale + scale * negative_cosine(t)
        weight[:, cols] = jnp.where(inside, -window, 0.0)

    @pl.loop(0, nfreq)
    def _(j):
        bins = freqs_ref[j] + (shift - HALF) * alpha_ref[0]
        base = pl.multiple_of(j * FREQ_ROWS, 16)
        turn = bins & 3
        even = jnp.where(turn == 0, 1.0, jnp.where(turn == 2, -1.0, 0.0))
        odd = jnp.where(turn == 1, 1.0, jnp.where(turn == 3, -1.0, 0.0))
        step = bins * (lane - first) + quarter
        here = negative_cosine(step)
        ahead = negative_cosine(step + NFFT // 4)

        def column(i, carry):
            here, ahead = carry
            cols = pl.ds(pl.multiple_of(i * 128, 128), 128)
            value = here * weight[:, cols]
            table[pl.ds(base, FREQ_ROWS), cols] = value.astype(jnp.bfloat16)
            return here * even + ahead * odd, ahead * even - here * odd

        lax.fori_loop(0, nt // 128, column, (here, ahead))

    for c in range(nchunk):
        own_copy(c).wait()

        @pl.loop(1, n)
        def _(k):
            peer = lax.rem(me + k, n)
            raw_copy(c, peer, peer).wait_recv()

        last = c == nchunk - 1

        @pl.loop(0, groups)
        def _(step):
            g = lax.rem(step + lax.div(me, GROUP) + groups // 2, groups)
            base = pl.multiple_of(g * (GROUP * FREQ_ROWS), 16)
            result = jnp.dot(
                table[pl.ds(base, GROUP * FREQ_ROWS), :],
                slabs[c][...],
                preferred_element_type=jnp.float32,
            ).astype(jnp.bfloat16)
            for i in range(GROUP):
                j = g * GROUP + i
                lines = result[i * FREQ_ROWS : i * FREQ_ROWS + GRAM_ROWS]
                first = i * FREQ_ROWS + GRAM_ROWS
                stage[c, j] = result[first : first + 2 * NBLK].reshape(NBLK, 2, width)
                product = lax.dot_general(
                    lines, lines, (((1,), (1,)), ((), ())), preferred_element_type=jnp.float32
                )
                if c > 0:
                    product += accum[j]
                if last:
                    pack_out[j] = packed(product)
                else:
                    accum[j] = product
            for i in range(GROUP):
                j = g * GROUP + i

                @pl.when(j != me)
                def _():
                    if last:
                        gram_copy(j, me).start()
                    spec_copy(c, j, me).start()

        own_spec_copy(c).start()

    pack_in[me] = pack_out[me]

    @pl.loop(1, n)
    def _(k):
        peer = lax.rem(me + k, n)
        gram_copy(peer, peer).wait_recv()

    total = pack_in[0].astype(jnp.float32)
    for p in range(1, n):
        total += pack_in[p].astype(jnp.float32)
    space_parts[my_space] = total

    @pl.loop(1, ns)
    def _(k):
        space_copy(lax.rem(my_space + k, ns), my_space).start()

    @pl.loop(1, ns)
    def _(k):
        peer = lax.rem(my_space + k, ns)
        pltpu.make_async_remote_copy(
            src_ref=space_parts.at[my_space],
            dst_ref=space_parts.at[peer],
            send_sem=space_send.at[peer],
            recv_sem=space_recv.at[peer],
            device_id=at_space(peer),
            device_id_type=MESH,
        ).wait_recv()

    total = space_parts[0]
    for p in range(1, ns):
        total += space_parts[p]
    total = total * (1.0 / total_cells)
    mixed = jnp.concatenate(
        [total, pltpu.roll(total, QUAD, 1), jnp.zeros((QUAD, 128), jnp.float32)], axis=0
    )
    flipped = mixed.T[:QUAD]
    mixed = mixed[:QUAD]
    real = jnp.where(prow <= pcol, mixed, flipped)
    imag = jnp.where(prow > pcol, mixed, jnp.where(prow == pcol, 0.0, -flipped))
    gram_ref[0, :, 0] = real[:ORDER, :ORDER]
    gram_ref[0, :, 1] = imag[:ORDER, :ORDER]

    for c in range(nchunk):
        own_spec_copy(c).wait()

        @pl.loop(1, n)
        def _(k):
            peer = lax.rem(me + k, n)
            spec_copy(c, peer, peer).wait_recv()

    for c in range(nchunk):

        @pl.loop(1, n)
        def _(k):
            peer = lax.rem(me + k, n)
            raw_copy(c, peer, me).wait_send()
            spec_copy(c, peer, me).wait_send()

    @pl.loop(1, n)
    def _(k):
        peer = lax.rem(me + k, n)
        gram_copy(peer, me).wait_send()

    @pl.loop(1, ns)
    def _(k):
        space_copy(lax.rem(my_space + k, ns), my_space).wait_send()


def hand_over(spec_in, gram_in, spec_out, gram_out, sems):
    copies = [
        pltpu.make_async_copy(spec_in, spec_out, sems.at[0]),
        pltpu.make_async_copy(gram_in, gram_out, sems.at[1]),
    ]
    for copy in copies:
        copy.start()
    for copy in copies:
        copy.wait()


def solution(mesh):
    n = mesh.shape["freq"]
    ns = mesh.shape["space"]

    def per_device(series, starts, freqs, alpha):
        rows, slab_cells = series.shape
        nfreq = freqs.shape[0]
        nt = rows * n
        own_cells = slab_cells // n
        nchunk = max(2, own_cells // 256)
        width = own_cells // nchunk
        smem = pl.BlockSpec(memory_space=pltpu.SMEM)
        table_rows = nfreq * FREQ_ROWS
        cost = pl.CostEstimate(
            flops=2 * table_rows * nt * own_cells,
            bytes_accessed=2 * rows * slab_cells * 2,
            transcendentals=0,
        )
        dma = pltpu.SemaphoreType.DMA
        spec, gram = pl.pallas_call(
            functools.partial(kernel, n, ns, nfreq, nchunk, slab_cells * ns),
            out_shape=(
                jax.ShapeDtypeStruct((NBLK, 2, slab_cells), jnp.bfloat16),
                jax.ShapeDtypeStruct((1, ORDER, 2, ORDER), jnp.float32),
            ),
            in_specs=[smem, smem, smem, pl.BlockSpec(memory_space=pl.ANY)],
            out_specs=(
                pl.BlockSpec(memory_space=pl.ANY),
                pl.BlockSpec(memory_space=pltpu.VMEM),
            ),
            scratch_shapes=[
                pltpu.VMEM((table_rows, nt), jnp.bfloat16),
                pltpu.VMEM((FREQ_ROWS, nt), jnp.float32),
                pltpu.VMEM((nchunk, nfreq, NBLK, 2, width), jnp.bfloat16),
                pltpu.VMEM((nchunk, n, rows, width), jnp.bfloat16),
                pltpu.VMEM((nfreq, GRAM_ROWS, GRAM_ROWS), jnp.float32),
                pltpu.VMEM((nfreq, QUAD // 2, 128), jnp.bfloat16),
                pltpu.VMEM((n, QUAD // 2, 128), jnp.bfloat16),
                pltpu.VMEM((ns, QUAD // 2, 128), jnp.float32),
                dma((nchunk, n)),
                dma((nchunk, n)),
                dma((nchunk, n)),
                dma((nchunk, n)),
                dma((n,)),
                dma((n,)),
                dma((ns,)),
                dma((ns,)),
                dma((2, nchunk)),
                dma((nchunk, n)),
            ]
            + [pltpu.VMEM((nt, width), jnp.bfloat16)] * nchunk,
            compiler_params=pltpu.CompilerParams(
                collective_id=0, has_side_effects=True, vmem_limit_bytes=60 * 1024 * 1024
            ),
            cost_estimate=cost,
        )(starts, freqs, alpha, series)
        anywhere = pl.BlockSpec(memory_space=pl.ANY)
        spec, gram = pl.pallas_call(
            hand_over,
            out_shape=(
                jax.ShapeDtypeStruct(spec.shape, spec.dtype),
                jax.ShapeDtypeStruct(gram.shape, gram.dtype),
            ),
            in_specs=[anywhere, anywhere],
            out_specs=(anywhere, anywhere),
            scratch_shapes=[dma((2,))],
            compiler_params=pltpu.CompilerParams(vmem_limit_bytes=60 * 1024 * 1024),
        )(spec, gram)
        own = jnp.transpose(spec, (1, 0, 2))
        return own[None], jnp.transpose(gram, (0, 2, 1, 3))

    placed = (P("freq", "space"), P(), P(), P())
    return jax.shard_map(
        per_device,
        mesh=mesh,
        in_specs=placed,
        out_specs=(P("freq", None, None, "space"), P("freq", None, None, None)),
        check_vma=False,
    )
```

```python
import functools
import math

import jax
import jax.numpy as jnp
from jax import lax
from jax.experimental import pallas as pl
from jax.experimental.pallas import tpu as pltpu
from jax.sharding import PartitionSpec as P

NFFT = 512
NBLK = 7
HALF = 4
SHIFTS = 9
ORDER = SHIFTS * NBLK
QUAD = 64
GRAM_ROWS = 2 * QUAD
OWN_ROWS = 16
FREQ_ROWS = GRAM_ROWS + OWN_ROWS
GROUP = 4
PARTS = 4
MESH = pl.DeviceIdType.MESH


def half_turn_sine(steps):
    x = steps.astype(jnp.float32) * (math.pi / 256.0)
    x2 = x * x
    p = -1.0 / math.factorial(11)
    for order in (9, 7, 5, 3, 1):
        p = p * x2 + (-1.0) ** ((order - 1) // 2) / math.factorial(order)
    return p * x


def negative_cosine(step):
    folded = 128 - jnp.abs((step & (NFFT - 1)) - NFFT // 2)
    return half_turn_sine(folded)


def row_fields(starts):
    row = lax.broadcasted_iota(jnp.int32, (FREQ_ROWS, 128), 0)
    own = row >= GRAM_ROWS
    part = jnp.where(own, row & 1, jnp.where(row >= QUAD, 1, 0))
    inner = jnp.where(own, (row - GRAM_ROWS) >> 1, row - QUAD * part)
    shift = jnp.zeros_like(row)
    for bound in range(1, SHIFTS + 1):
        shift += jnp.where(inner >= NBLK * bound, 1, 0)
    block = jnp.where(own, inner, inner - NBLK * shift)
    used = inner < jnp.where(own, NBLK, ORDER)
    shift = jnp.where(own, HALF, shift)
    first = jnp.zeros_like(row)
    for index in range(NBLK):
        first = jnp.where(block == index, starts[index], first)
    return shift, part, first, used


def kernel(
    n,
    ns,
    nfreq,
    nchunk,
    total_cells,
    starts_ref,
    freqs_ref,
    alpha_ref,
    series_ref,
    spec_ref,
    gram_ref,
    table,
    weight,
    stage,
    outgoing,
    sums,
    accum,
    pack_out,
    pack_in,
    space_parts,
    raw_send,
    raw_recv,
    spec_send,
    spec_recv,
    gram_send,
    gram_recv,
    space_send,
    space_recv,
    local_sem,
    stage_sem,
    *slabs,
):
    me = lax.axis_index("freq")
    my_space = lax.axis_index("space")
    rows, slab_cells = series_ref.shape
    nt = rows * n
    own_cells = slab_cells // n
    width = own_cells // nchunk

    def at_freq(peer):
        return {"freq": peer, "space": my_space}

    def at_space(peer):
        return {"freq": me, "space": peer}

    def stage_copy(c, peer):
        cells = pl.ds(pl.multiple_of(peer * own_cells + c * width, 128), width)
        return pltpu.make_async_copy(
            series_ref.at[:, cells], outgoing.at[c, peer], stage_sem.at[c, peer]
        )

    def peer_at(k):
        return lax.rem(me + 1 + lax.rem(k + n // 2 - 1, n - 1), n)

    barrier = pltpu.get_barrier_semaphore()

    @pl.loop(1, n)
    def _(k):
        pl.semaphore_signal(
            barrier, inc=1, device_id=at_freq(lax.rem(me + k, n)), device_id_type=MESH
        )

    @pl.loop(1, ns)
    def _(k):
        pl.semaphore_signal(
            barrier, inc=1, device_id=at_space(lax.rem(my_space + k, ns)), device_id_type=MESH
        )

    for c in range(nchunk):

        @pl.loop(0, n - 1)
        def _(k):
            stage_copy(c, peer_at(k)).start()

    pl.semaphore_wait(barrier, n + ns - 2)

    def raw_copy(c, peer, slot):
        mine = pl.ds(pl.multiple_of(me * rows, rows), rows)
        return pltpu.make_async_remote_copy(
            src_ref=outgoing.at[c, peer],
            dst_ref=slabs[c].at[mine, :],
            send_sem=raw_send.at[c, peer],
            recv_sem=raw_recv.at[c, slot],
            device_id=at_freq(peer),
            device_id_type=MESH,
        )

    def own_copy(c):
        cells = pl.ds(pl.multiple_of(me * own_cells + c * width, 128), width)
        mine = pl.ds(pl.multiple_of(me * rows, rows), rows)
        return pltpu.make_async_copy(
            series_ref.at[:, cells], slabs[c].at[mine, :], local_sem.at[0, c]
        )

    def spec_copy(c, peer, slot):
        cells = pl.ds(pl.multiple_of(me * own_cells + c * width, 128), width)
        return pltpu.make_async_remote_copy(
            src_ref=stage.at[c, peer],
            dst_ref=spec_ref.at[:, :, cells],
            send_sem=spec_send.at[c, peer],
            recv_sem=spec_recv.at[c, slot],
            device_id=at_freq(peer),
            device_id_type=MESH,
        )

    def own_spec_copy(c):
        cells = pl.ds(pl.multiple_of(me * own_cells + c * width, 128), width)
        return pltpu.make_async_copy(
            stage.at[c, me], spec_ref.at[:, :, cells], local_sem.at[1, c]
        )

    def gram_copy(peer, slot):
        return pltpu.make_async_remote_copy(
            src_ref=pack_out.at[peer],
            dst_ref=pack_in.at[me],
            send_sem=gram_send.at[peer],
            recv_sem=gram_recv.at[slot],
            device_id=at_freq(peer),
            device_id_type=MESH,
        )

    def space_copy(peer, slot):
        return pltpu.make_async_remote_copy(
            src_ref=space_parts.at[my_space],
            dst_ref=space_parts.at[my_space],
            send_sem=space_send.at[peer],
            recv_sem=space_recv.at[slot],
            device_id=at_space(peer),
            device_id_type=MESH,
        )

    for c in range(nchunk):

        @pl.loop(0, n - 1)
        def _(k):
            peer = peer_at(k)
            stage_copy(c, peer).wait()
            raw_copy(c, peer, me).start()

        own_copy(c).start()

    groups = nfreq // GROUP
    prow = lax.broadcasted_iota(jnp.int32, (QUAD, 128), 0)
    pcol = lax.broadcasted_iota(jnp.int32, (QUAD, 128), 1)
    left = lax.broadcasted_iota(jnp.int32, (QUAD // 2, 128), 1) < QUAD

    def packed(whole):
        turned = pltpu.roll(whole, QUAD, 1)
        real = whole[:QUAD] + turned[QUAD:]
        imag = turned[:QUAD] - whole[QUAD:]
        mixed = jnp.where(prow <= pcol, real, imag)
        low = pltpu.roll(mixed[QUAD // 2 :], QUAD, 1)
        return jnp.where(left, mixed[: QUAD // 2], low).astype(jnp.bfloat16)

    shift, part, first, used = row_fields([starts_ref[b] for b in range(NBLK)])
    quarter = part * (NFFT // 4)
    scale = 0.5 / math.sqrt(0.375 * NFFT)
    lane = lax.broadcasted_iota(jnp.int32, (FREQ_ROWS, 128), 1)

    @pl.loop(0, nt // 128)
    def _(i):
        cols = pl.ds(pl.multiple_of(i * 128, 128), 128)
        t = lane + i * 128 - first
        inside = (t >= 0) & (t < NFFT) & used
        window = scale + scale * negative_cosine(t)
        weight[:, cols] = jnp.where(inside, -window, 0.0)

    @pl.loop(0, nfreq)
    def _(j):
        bins = freqs_ref[j] + (shift - HALF) * alpha_ref[0]
        base = pl.multiple_of(j * FREQ_ROWS, 16)
        turn = bins & 3
        even = jnp.where(turn == 0, 1.0, jnp.where(turn == 2, -1.0, 0.0))
        odd = jnp.where(turn == 1, 1.0, jnp.where(turn == 3, -1.0, 0.0))
        step = bins * (lane - first) + quarter
        here = negative_cosine(step)
        ahead = negative_cosine(step + NFFT // 4)

        def column(i, carry):
            here, ahead = carry
            cols = pl.ds(pl.multiple_of(i * 128, 128), 128)
            value = here * weight[:, cols]
            table[pl.ds(base, FREQ_ROWS), cols] = value.astype(jnp.bfloat16)
            return here * even + ahead * odd, ahead * even - here * odd

        lax.fori_loop(0, nt // 128, column, (here, ahead))

    def far_first(step, count):
        return lax.rem(step + lax.div(me * count, n) + count // 2, count)

    def table_rows(g):
        return pl.ds(pl.multiple_of(g * (GROUP * FREQ_ROWS), 16), GROUP * FREQ_ROWS)

    def correlate(c, g, result):
        result = result.astype(jnp.bfloat16)
        for i in range(GROUP):
            j = g * GROUP + i
            lines = result[i * FREQ_ROWS : i * FREQ_ROWS + GRAM_ROWS]
            own = i * FREQ_ROWS + GRAM_ROWS
            stage[c, j] = result[own : own + 2 * NBLK].reshape(NBLK, 2, width)
            product = lax.dot_general(
                lines, lines, (((1,), (1,)), ((), ())), preferred_element_type=jnp.float32
            )
            if c > 0:
                product += accum[j]
            if c == nchunk - 1:
                pack_out[j] = packed(product)
            else:
                accum[j] = product

    def send_spectra(c):
        @pl.loop(0, n - 1)
        def _(k):
            spec_copy(c, peer_at(k), me).start()

        own_spec_copy(c).start()

    for c in range(nchunk - 1):
        own_copy(c).wait()

        @pl.loop(1, n)
        def _(k):
            peer = lax.rem(me + k, n)
            raw_copy(c, peer, peer).wait_recv()

        @pl.loop(0, groups)
        def _(g):
            result = jnp.dot(
                table[table_rows(g), :], slabs[c][...], preferred_element_type=jnp.float32
            )
            correlate(c, g, result)

        send_spectra(c)

    c = nchunk - 1
    sources = n // PARTS
    for q in range(PARTS):
        part_index = far_first(q, PARTS)

        @pl.loop(0, sources)
        def _(i):
            peer = part_index * sources + i

            @pl.when(peer != me)
            def _():
                raw_copy(c, peer, peer).wait_recv()

            @pl.when(peer == me)
            def _():
                own_copy(c).wait()

        span = pl.ds(pl.multiple_of(part_index * (nt // PARTS), 128), nt // PARTS)

        @pl.loop(0, groups)
        def _(step):
            g = far_first(step, groups)
            result = jnp.dot(
                table[table_rows(g), span], slabs[c][span, :], preferred_element_type=jnp.float32
            )
            if q > 0:
                result += sums[table_rows(g), :]
            if q < PARTS - 1:
                sums[table_rows(g), :] = result
            else:
                correlate(c, g, result)
                for i in range(GROUP):
                    j = g * GROUP + i

                    @pl.when(j != me)
                    def _():
                        gram_copy(j, me).start()

    send_spectra(c)

    pack_in[me] = pack_out[me]

    @pl.loop(1, n)
    def _(k):
        peer = lax.rem(me + k, n)
        gram_copy(peer, peer).wait_recv()

    total = pack_in[0].astype(jnp.float32)
    for p in range(1, n):
        total += pack_in[p].astype(jnp.float32)
    space_parts[my_space] = total

    @pl.loop(1, ns)
    def _(k):
        space_copy(lax.rem(my_space + k, ns), my_space).start()

    @pl.loop(1, ns)
    def _(k):
        peer = lax.rem(my_space + k, ns)
        pltpu.make_async_remote_copy(
            src_ref=space_parts.at[my_space],
            dst_ref=space_parts.at[peer],
            send_sem=space_send.at[peer],
            recv_sem=space_recv.at[peer],
            device_id=at_space(peer),
            device_id_type=MESH,
        ).wait_recv()

    total = space_parts[0]
    for p in range(1, ns):
        total += space_parts[p]
    total = total * (1.0 / total_cells)
    mixed = jnp.concatenate(
        [total, pltpu.roll(total, QUAD, 1), jnp.zeros((QUAD, 128), jnp.float32)], axis=0
    )
    flipped = mixed.T[:QUAD]
    mixed = mixed[:QUAD]
    real = jnp.where(prow <= pcol, mixed, flipped)
    imag = jnp.where(prow > pcol, mixed, jnp.where(prow == pcol, 0.0, -flipped))
    gram_ref[0, :, 0] = real[:ORDER, :ORDER]
    gram_ref[0, :, 1] = imag[:ORDER, :ORDER]

    for c in range(nchunk):
        own_spec_copy(c).wait()

        @pl.loop(1, n)
        def _(k):
            peer = lax.rem(me + k, n)
            spec_copy(c, peer, peer).wait_recv()

    for c in range(nchunk):

        @pl.loop(1, n)
        def _(k):
            peer = lax.rem(me + k, n)
            raw_copy(c, peer, me).wait_send()
            spec_copy(c, peer, me).wait_send()

    @pl.loop(1, n)
    def _(k):
        peer = lax.rem(me + k, n)
        gram_copy(peer, me).wait_send()

    @pl.loop(1, ns)
    def _(k):
        space_copy(lax.rem(my_space + k, ns), my_space).wait_send()


def solution(mesh):
    n = mesh.shape["freq"]
    ns = mesh.shape["space"]

    def per_device(series, starts, freqs, alpha):
        rows, slab_cells = series.shape
        nfreq = freqs.shape[0]
        nt = rows * n
        own_cells = slab_cells // n
        nchunk = max(2, own_cells // 256)
        width = own_cells // nchunk
        smem = pl.BlockSpec(memory_space=pltpu.SMEM)
        table_rows = nfreq * FREQ_ROWS
        cost = pl.CostEstimate(
            flops=2 * table_rows * nt * own_cells,
            bytes_accessed=2 * rows * slab_cells * 2,
            transcendentals=0,
        )
        dma = pltpu.SemaphoreType.DMA
        spec, gram = pl.pallas_call(
            functools.partial(kernel, n, ns, nfreq, nchunk, slab_cells * ns),
            out_shape=(
                jax.ShapeDtypeStruct((NBLK, 2, slab_cells), jnp.bfloat16),
                jax.ShapeDtypeStruct((1, ORDER, 2, ORDER), jnp.float32),
            ),
            in_specs=[smem, smem, smem, pl.BlockSpec(memory_space=pl.ANY)],
            out_specs=(
                pl.BlockSpec(memory_space=pl.ANY),
                pl.BlockSpec(memory_space=pltpu.VMEM),
            ),
            scratch_shapes=[
                pltpu.VMEM((table_rows, nt), jnp.bfloat16),
                pltpu.VMEM((FREQ_ROWS, nt), jnp.float32),
                pltpu.VMEM((nchunk, nfreq, NBLK, 2, width), jnp.bfloat16),
                pltpu.VMEM((nchunk, n, rows, width), jnp.bfloat16),
                pltpu.VMEM((table_rows, width), jnp.float32),
                pltpu.VMEM((nfreq, GRAM_ROWS, GRAM_ROWS), jnp.float32),
                pltpu.VMEM((nfreq, QUAD // 2, 128), jnp.bfloat16),
                pltpu.VMEM((n, QUAD // 2, 128), jnp.bfloat16),
                pltpu.VMEM((ns, QUAD // 2, 128), jnp.float32),
                dma((nchunk, n)),
                dma((nchunk, n)),
                dma((nchunk, n)),
                dma((nchunk, n)),
                dma((n,)),
                dma((n,)),
                dma((ns,)),
                dma((ns,)),
                dma((2, nchunk)),
                dma((nchunk, n)),
            ]
            + [pltpu.VMEM((nt, width), jnp.bfloat16)] * nchunk,
            compiler_params=pltpu.CompilerParams(
                collective_id=0, has_side_effects=True, vmem_limit_bytes=60 * 1024 * 1024
            ),
            cost_estimate=cost,
        )(starts, freqs, alpha, series)
        own = jnp.transpose(spec, (1, 0, 2))
        return own[None], jnp.transpose(gram, (0, 2, 1, 3))

    placed = (P("freq", "space"), P(), P(), P())
    return jax.shard_map(
        per_device,
        mesh=mesh,
        in_specs=placed,
        out_specs=(P("freq", None, None, "space"), P("freq", None, None, None)),
        check_vma=False,
    )
```

```python
import functools
import math

import jax
import jax.numpy as jnp
from jax import lax
from jax.experimental import pallas as pl
from jax.experimental.pallas import tpu as pltpu
from jax.sharding import PartitionSpec as P

NFFT = 512
NBLK = 7
HALF = 4
SHIFTS = 9
ORDER = SHIFTS * NBLK
QUAD = 64
GRAM_ROWS = 2 * QUAD
OWN_ROWS = 16
FREQ_ROWS = GRAM_ROWS + OWN_ROWS
GROUP = 4
PARTS = 4
MESH = pl.DeviceIdType.MESH


def half_turn_sine(steps):
    x = steps.astype(jnp.float32) * (math.pi / 256.0)
    x2 = x * x
    p = -1.0 / math.factorial(11)
    for order in (9, 7, 5, 3, 1):
        p = p * x2 + (-1.0) ** ((order - 1) // 2) / math.factorial(order)
    return p * x


def negative_cosine(step):
    folded = 128 - jnp.abs((step & (NFFT - 1)) - NFFT // 2)
    return half_turn_sine(folded)


def row_fields(starts):
    row = lax.broadcasted_iota(jnp.int32, (FREQ_ROWS, 128), 0)
    own = row >= GRAM_ROWS
    part = jnp.where(own, row & 1, jnp.where(row >= QUAD, 1, 0))
    inner = jnp.where(own, (row - GRAM_ROWS) >> 1, row - QUAD * part)
    shift = jnp.zeros_like(row)
    for bound in range(1, SHIFTS + 1):
        shift += jnp.where(inner >= NBLK * bound, 1, 0)
    block = jnp.where(own, inner, inner - NBLK * shift)
    used = inner < jnp.where(own, NBLK, ORDER)
    shift = jnp.where(own, HALF, shift)
    first = jnp.zeros_like(row)
    for index in range(NBLK):
        first = jnp.where(block == index, starts[index], first)
    return shift, part, first, used


def kernel(
    n,
    ns,
    nfreq,
    nchunk,
    total_cells,
    starts_ref,
    freqs_ref,
    alpha_ref,
    series_ref,
    spec_ref,
    gram_ref,
    table,
    weight,
    stage,
    outgoing,
    sums,
    accum,
    pack_out,
    pack_in,
    space_parts,
    raw_send,
    raw_recv,
    spec_send,
    spec_recv,
    gram_send,
    gram_recv,
    space_send,
    space_recv,
    local_sem,
    stage_sem,
    *slabs,
):
    me = lax.axis_index("freq")
    my_space = lax.axis_index("space")
    rows, slab_cells = series_ref.shape
    nt = rows * n
    own_cells = slab_cells // n
    width = own_cells // nchunk

    def at_freq(peer):
        return {"freq": peer, "space": my_space}

    def at_space(peer):
        return {"freq": me, "space": peer}

    def stage_copy(c, peer):
        cells = pl.ds(pl.multiple_of(peer * own_cells + c * width, 128), width)
        return pltpu.make_async_copy(
            series_ref.at[:, cells], outgoing.at[c, peer], stage_sem.at[c, peer]
        )

    def peer_at(k):
        return lax.rem(me + 1 + lax.rem(k + n // 2 - 1, n - 1), n)

    barrier = pltpu.get_barrier_semaphore()

    @pl.loop(1, n)
    def _(k):
        pl.semaphore_signal(
            barrier, inc=1, device_id=at_freq(lax.rem(me + k, n)), device_id_type=MESH
        )

    @pl.loop(1, ns)
    def _(k):
        pl.semaphore_signal(
            barrier, inc=1, device_id=at_space(lax.rem(my_space + k, ns)), device_id_type=MESH
        )

    for c in range(nchunk):

        @pl.loop(0, n - 1)
        def _(k):
            stage_copy(c, peer_at(k)).start()

    pl.semaphore_wait(barrier, n + ns - 2)

    def raw_copy(c, peer, slot):
        mine = pl.ds(pl.multiple_of(me * rows, rows), rows)
        return pltpu.make_async_remote_copy(
            src_ref=outgoing.at[c, peer],
            dst_ref=slabs[c].at[mine, :],
            send_sem=raw_send.at[c, peer],
            recv_sem=raw_recv.at[c, slot],
            device_id=at_freq(peer),
            device_id_type=MESH,
        )

    def own_copy(c):
        cells = pl.ds(pl.multiple_of(me * own_cells + c * width, 128), width)
        mine = pl.ds(pl.multiple_of(me * rows, rows), rows)
        return pltpu.make_async_copy(
            series_ref.at[:, cells], slabs[c].at[mine, :], local_sem.at[0, c]
        )

    def spec_copy(c, peer, slot):
        cells = pl.ds(pl.multiple_of(me * own_cells + c * width, 128), width)
        return pltpu.make_async_remote_copy(
            src_ref=stage.at[c, peer],
            dst_ref=spec_ref.at[:, :, cells],
            send_sem=spec_send.at[c, peer],
            recv_sem=spec_recv.at[c, slot],
            device_id=at_freq(peer),
            device_id_type=MESH,
        )

    def own_spec_copy(c):
        cells = pl.ds(pl.multiple_of(me * own_cells + c * width, 128), width)
        return pltpu.make_async_copy(
            stage.at[c, me], spec_ref.at[:, :, cells], local_sem.at[1, c]
        )

    def gram_copy(peer, slot):
        return pltpu.make_async_remote_copy(
            src_ref=pack_out.at[peer],
            dst_ref=pack_in.at[me],
            send_sem=gram_send.at[peer],
            recv_sem=gram_recv.at[slot],
            device_id=at_freq(peer),
            device_id_type=MESH,
        )

    def space_copy(peer, slot):
        return pltpu.make_async_remote_copy(
            src_ref=space_parts.at[my_space],
            dst_ref=space_parts.at[my_space],
            send_sem=space_send.at[peer],
            recv_sem=space_recv.at[slot],
            device_id=at_space(peer),
            device_id_type=MESH,
        )

    for c in range(nchunk):

        @pl.loop(0, n - 1)
        def _(k):
            peer = peer_at(k)
            stage_copy(c, peer).wait()
            raw_copy(c, peer, me).start()

        own_copy(c).start()

    groups = nfreq // GROUP
    prow = lax.broadcasted_iota(jnp.int32, (QUAD, 128), 0)
    pcol = lax.broadcasted_iota(jnp.int32, (QUAD, 128), 1)
    left = lax.broadcasted_iota(jnp.int32, (QUAD // 2, 128), 1) < QUAD

    def packed(whole):
        turned = pltpu.roll(whole, QUAD, 1)
        real = whole[:QUAD] + turned[QUAD:]
        imag = turned[:QUAD] - whole[QUAD:]
        mixed = jnp.where(prow <= pcol, real, imag)
        low = pltpu.roll(mixed[QUAD // 2 :], QUAD, 1)
        return jnp.where(left, mixed[: QUAD // 2], low).astype(jnp.bfloat16)

    shift, part, first, used = row_fields([starts_ref[b] for b in range(NBLK)])
    quarter = part * (NFFT // 4)
    scale = 0.5 / math.sqrt(0.375 * NFFT)
    lane = lax.broadcasted_iota(jnp.int32, (FREQ_ROWS, 128), 1)

    @pl.loop(0, nt // 128)
    def _(i):
        cols = pl.ds(pl.multiple_of(i * 128, 128), 128)
        t = lane + i * 128 - first
        inside = (t >= 0) & (t < NFFT) & used
        window = scale + scale * negative_cosine(t)
        weight[:, cols] = jnp.where(inside, -window, 0.0)

    @pl.loop(0, nfreq)
    def _(j):
        bins = freqs_ref[j] + (shift - HALF) * alpha_ref[0]
        base = pl.multiple_of(j * FREQ_ROWS, 16)
        turn = bins & 3
        even = jnp.where(turn == 0, 1.0, jnp.where(turn == 2, -1.0, 0.0))
        odd = jnp.where(turn == 1, 1.0, jnp.where(turn == 3, -1.0, 0.0))
        step = bins * (lane - first) + quarter
        here = negative_cosine(step)
        ahead = negative_cosine(step + NFFT // 4)

        def column(i, carry):
            here, ahead = carry
            cols = pl.ds(pl.multiple_of(i * 128, 128), 128)
            value = here * weight[:, cols]
            table[pl.ds(base, FREQ_ROWS), cols] = value.astype(jnp.bfloat16)
            return here * even + ahead * odd, ahead * even - here * odd

        lax.fori_loop(0, nt // 128, column, (here, ahead))

    def far_first(step, count):
        return lax.rem(step + lax.div(me * count, n) + count // 2, count)

    def table_rows(g):
        return pl.ds(pl.multiple_of(g * (GROUP * FREQ_ROWS), 16), GROUP * FREQ_ROWS)

    def correlate(c, g, result):
        result = result.astype(jnp.bfloat16)
        for i in range(GROUP):
            j = g * GROUP + i
            lines = result[i * FREQ_ROWS : i * FREQ_ROWS + GRAM_ROWS]
            own = i * FREQ_ROWS + GRAM_ROWS
            stage[c, j] = result[own : own + 2 * NBLK].reshape(NBLK, 2, width)
            product = lax.dot_general(
                lines, lines, (((1,), (1,)), ((), ())), preferred_element_type=jnp.float32
            )
            if c > 0:
                product += accum[j]
            if c == nchunk - 1:
                pack_out[j] = packed(product)
            else:
                accum[j] = product

    def send_spectra(c):
        @pl.loop(0, n - 1)
        def _(k):
            spec_copy(c, peer_at(k), me).start()

        own_spec_copy(c).start()

    for c in range(nchunk - 1):
        own_copy(c).wait()

        @pl.loop(1, n)
        def _(k):
            peer = lax.rem(me + k, n)
            raw_copy(c, peer, peer).wait_recv()

        @pl.loop(0, groups)
        def _(g):
            result = jnp.dot(
                table[table_rows(g), :], slabs[c][...], preferred_element_type=jnp.float32
            )
            correlate(c, g, result)

        send_spectra(c)

    c = nchunk - 1
    sources = n // PARTS
    for q in range(PARTS):
        part_index = far_first(q, PARTS)

        @pl.loop(0, sources)
        def _(i):
            peer = part_index * sources + i

            @pl.when(peer != me)
            def _():
                raw_copy(c, peer, peer).wait_recv()

            @pl.when(peer == me)
            def _():
                own_copy(c).wait()

        span = pl.ds(pl.multiple_of(part_index * (nt // PARTS), 128), nt // PARTS)

        @pl.loop(0, groups)
        def _(step):
            g = far_first(step, groups)
            result = jnp.dot(
                table[table_rows(g), span], slabs[c][span, :], preferred_element_type=jnp.float32
            )
            if q > 0:
                result += sums[table_rows(g), :]
            if q < PARTS - 1:
                sums[table_rows(g), :] = result
            else:
                correlate(c, g, result)
                for i in range(GROUP):
                    j = g * GROUP + i

                    @pl.when(j != me)
                    def _():
                        gram_copy(j, me).start()

    send_spectra(c)

    pack_in[me] = pack_out[me]

    @pl.loop(1, n)
    def _(k):
        peer = lax.rem(me + k, n)
        gram_copy(peer, peer).wait_recv()

    total = pack_in[0].astype(jnp.float32)
    for p in range(1, n):
        total += pack_in[p].astype(jnp.float32)
    space_parts[my_space] = total

    @pl.loop(1, ns)
    def _(k):
        space_copy(lax.rem(my_space + k, ns), my_space).start()

    @pl.loop(1, ns)
    def _(k):
        peer = lax.rem(my_space + k, ns)
        pltpu.make_async_remote_copy(
            src_ref=space_parts.at[my_space],
            dst_ref=space_parts.at[peer],
            send_sem=space_send.at[peer],
            recv_sem=space_recv.at[peer],
            device_id=at_space(peer),
            device_id_type=MESH,
        ).wait_recv()

    total = space_parts[0]
    for p in range(1, ns):
        total += space_parts[p]
    total = total * (1.0 / total_cells)
    mixed = jnp.concatenate(
        [total, pltpu.roll(total, QUAD, 1), jnp.zeros((QUAD, 128), jnp.float32)], axis=0
    )
    flipped = mixed.T[:QUAD]
    mixed = mixed[:QUAD]
    real = jnp.where(prow <= pcol, mixed, flipped)
    imag = jnp.where(prow > pcol, mixed, jnp.where(prow == pcol, 0.0, -flipped))
    gram_ref[0, :, 0] = real[:ORDER, :ORDER]
    gram_ref[0, :, 1] = imag[:ORDER, :ORDER]

    for c in range(nchunk):
        own_spec_copy(c).wait()

        @pl.loop(1, n)
        def _(k):
            peer = lax.rem(me + k, n)
            spec_copy(c, peer, peer).wait_recv()

    for c in range(nchunk):

        @pl.loop(1, n)
        def _(k):
            peer = lax.rem(me + k, n)
            raw_copy(c, peer, me).wait_send()
            spec_copy(c, peer, me).wait_send()

    @pl.loop(1, n)
    def _(k):
        peer = lax.rem(me + k, n)
        gram_copy(peer, me).wait_send()

    @pl.loop(1, ns)
    def _(k):
        space_copy(lax.rem(my_space + k, ns), my_space).wait_send()


def solution(mesh):
    n = mesh.shape["freq"]
    ns = mesh.shape["space"]

    def per_device(series, starts, freqs, alpha):
        rows, slab_cells = series.shape
        nfreq = freqs.shape[0]
        nt = rows * n
        own_cells = slab_cells // n
        nchunk = max(2, own_cells // 512)
        width = own_cells // nchunk
        smem = pl.BlockSpec(memory_space=pltpu.SMEM)
        table_rows = nfreq * FREQ_ROWS
        cost = pl.CostEstimate(
            flops=2 * table_rows * nt * own_cells,
            bytes_accessed=2 * rows * slab_cells * 2,
            transcendentals=0,
        )
        dma = pltpu.SemaphoreType.DMA
        spec, gram = pl.pallas_call(
            functools.partial(kernel, n, ns, nfreq, nchunk, slab_cells * ns),
            out_shape=(
                jax.ShapeDtypeStruct((NBLK, 2, slab_cells), jnp.bfloat16),
                jax.ShapeDtypeStruct((1, ORDER, 2, ORDER), jnp.float32),
            ),
            in_specs=[smem, smem, smem, pl.BlockSpec(memory_space=pl.ANY)],
            out_specs=(
                pl.BlockSpec(memory_space=pl.ANY),
                pl.BlockSpec(memory_space=pltpu.VMEM),
            ),
            scratch_shapes=[
                pltpu.VMEM((table_rows, nt), jnp.bfloat16),
                pltpu.VMEM((FREQ_ROWS, nt), jnp.float32),
                pltpu.VMEM((nchunk, nfreq, NBLK, 2, width), jnp.bfloat16),
                pltpu.VMEM((nchunk, n, rows, width), jnp.bfloat16),
                pltpu.VMEM((table_rows, width), jnp.float32),
                pltpu.VMEM((nfreq, GRAM_ROWS, GRAM_ROWS), jnp.float32),
                pltpu.VMEM((nfreq, QUAD // 2, 128), jnp.bfloat16),
                pltpu.VMEM((n, QUAD // 2, 128), jnp.bfloat16),
                pltpu.VMEM((ns, QUAD // 2, 128), jnp.float32),
                dma((nchunk, n)),
                dma((nchunk, n)),
                dma((nchunk, n)),
                dma((nchunk, n)),
                dma((n,)),
                dma((n,)),
                dma((ns,)),
                dma((ns,)),
                dma((2, nchunk)),
                dma((nchunk, n)),
            ]
            + [pltpu.VMEM((nt, width), jnp.bfloat16)] * nchunk,
            compiler_params=pltpu.CompilerParams(
                collective_id=0, has_side_effects=True, vmem_limit_bytes=60 * 1024 * 1024
            ),
            cost_estimate=cost,
        )(starts, freqs, alpha, series)
        own = jnp.transpose(spec, (1, 0, 2))
        return own[None], jnp.transpose(gram, (0, 2, 1, 3))

    placed = (P("freq", "space"), P(), P(), P())
    return jax.shard_map(
        per_device,
        mesh=mesh,
        in_specs=placed,
        out_specs=(P("freq", None, None, "space"), P("freq", None, None, None)),
        check_vma=False,
    )
```

```python
import functools
import math

import jax
import jax.numpy as jnp
from jax import lax
from jax.experimental import pallas as pl
from jax.experimental.pallas import tpu as pltpu
from jax.sharding import PartitionSpec as P

NFFT = 512
NBLK = 7
HALF = 4
SHIFTS = 9
ORDER = SHIFTS * NBLK
QUAD = 64
GRAM_ROWS = 2 * QUAD
OWN_ROWS = 16
FREQ_ROWS = GRAM_ROWS + OWN_ROWS
GROUP = 4
PARTS = 4
MESH = pl.DeviceIdType.MESH


def half_turn_sine(steps):
    x = steps.astype(jnp.float32) * (math.pi / 256.0)
    x2 = x * x
    p = -1.0 / math.factorial(11)
    for order in (9, 7, 5, 3, 1):
        p = p * x2 + (-1.0) ** ((order - 1) // 2) / math.factorial(order)
    return p * x


def negative_cosine(step):
    folded = 128 - jnp.abs((step & (NFFT - 1)) - NFFT // 2)
    return half_turn_sine(folded)


def row_fields(starts):
    row = lax.broadcasted_iota(jnp.int32, (FREQ_ROWS, 128), 0)
    own = row >= GRAM_ROWS
    part = jnp.where(own, row & 1, jnp.where(row >= QUAD, 1, 0))
    inner = jnp.where(own, (row - GRAM_ROWS) >> 1, row - QUAD * part)
    shift = jnp.zeros_like(row)
    for bound in range(1, SHIFTS + 1):
        shift += jnp.where(inner >= NBLK * bound, 1, 0)
    block = jnp.where(own, inner, inner - NBLK * shift)
    used = inner < jnp.where(own, NBLK, ORDER)
    shift = jnp.where(own, HALF, shift)
    first = jnp.zeros_like(row)
    for index in range(NBLK):
        first = jnp.where(block == index, starts[index], first)
    return shift, part, first, used


def kernel(
    n,
    ns,
    nfreq,
    nchunk,
    total_cells,
    starts_ref,
    freqs_ref,
    alpha_ref,
    series_ref,
    spec_ref,
    gram_ref,
    table,
    weight,
    stage,
    outgoing,
    sums,
    accum,
    pack_out,
    pack_in,
    space_parts,
    raw_send,
    raw_recv,
    spec_send,
    spec_recv,
    gram_send,
    gram_recv,
    space_send,
    space_recv,
    local_sem,
    stage_sem,
    *slabs,
):
    me = lax.axis_index("freq")
    my_space = lax.axis_index("space")
    rows, slab_cells = series_ref.shape
    nt = rows * n
    own_cells = slab_cells // n
    width = own_cells // nchunk

    def at_freq(peer):
        return {"freq": peer, "space": my_space}

    def at_space(peer):
        return {"freq": me, "space": peer}

    def stage_copy(c, peer):
        cells = pl.ds(pl.multiple_of(peer * own_cells + c * width, 128), width)
        return pltpu.make_async_copy(
            series_ref.at[:, cells], outgoing.at[c, peer], stage_sem.at[c, peer]
        )

    half = n // 2
    place = lax.rem(me, half)

    def peer_at(k):
        far = half - (me - place) + lax.rem(place + lax.div(k, 2), half)
        near = me - place + lax.rem(place + 1 + lax.div(k, 2), half)
        return far + lax.rem(k, 2) * (near - far)

    barrier = pltpu.get_barrier_semaphore()

    @pl.loop(1, n)
    def _(k):
        pl.semaphore_signal(
            barrier, inc=1, device_id=at_freq(lax.rem(me + k, n)), device_id_type=MESH
        )

    @pl.loop(1, ns)
    def _(k):
        pl.semaphore_signal(
            barrier, inc=1, device_id=at_space(lax.rem(my_space + k, ns)), device_id_type=MESH
        )

    for c in range(nchunk):

        @pl.loop(0, n - 1)
        def _(k):
            stage_copy(c, peer_at(k)).start()

    pl.semaphore_wait(barrier, n + ns - 2)

    def raw_copy(c, peer, slot):
        mine = pl.ds(pl.multiple_of(me * rows, rows), rows)
        return pltpu.make_async_remote_copy(
            src_ref=outgoing.at[c, peer],
            dst_ref=slabs[c].at[mine, :],
            send_sem=raw_send.at[c, peer],
            recv_sem=raw_recv.at[c, slot],
            device_id=at_freq(peer),
            device_id_type=MESH,
        )

    def own_copy(c):
        cells = pl.ds(pl.multiple_of(me * own_cells + c * width, 128), width)
        mine = pl.ds(pl.multiple_of(me * rows, rows), rows)
        return pltpu.make_async_copy(
            series_ref.at[:, cells], slabs[c].at[mine, :], local_sem.at[0, c]
        )

    def spec_copy(c, peer, slot):
        cells = pl.ds(pl.multiple_of(me * own_cells + c * width, 128), width)
        return pltpu.make_async_remote_copy(
            src_ref=stage.at[c, peer],
            dst_ref=spec_ref.at[:, :, cells],
            send_sem=spec_send.at[c, peer],
            recv_sem=spec_recv.at[c, slot],
            device_id=at_freq(peer),
            device_id_type=MESH,
        )

    def own_spec_copy(c):
        cells = pl.ds(pl.multiple_of(me * own_cells + c * width, 128), width)
        return pltpu.make_async_copy(
            stage.at[c, me], spec_ref.at[:, :, cells], local_sem.at[1, c]
        )

    def gram_copy(peer, slot):
        return pltpu.make_async_remote_copy(
            src_ref=pack_out.at[peer],
            dst_ref=pack_in.at[me],
            send_sem=gram_send.at[peer],
            recv_sem=gram_recv.at[slot],
            device_id=at_freq(peer),
            device_id_type=MESH,
        )

    def space_copy(peer, slot):
        return pltpu.make_async_remote_copy(
            src_ref=space_parts.at[my_space],
            dst_ref=space_parts.at[my_space],
            send_sem=space_send.at[peer],
            recv_sem=space_recv.at[slot],
            device_id=at_space(peer),
            device_id_type=MESH,
        )

    for c in range(nchunk):

        @pl.loop(0, n - 1)
        def _(k):
            peer = peer_at(k)
            stage_copy(c, peer).wait()
            raw_copy(c, peer, me).start()

        own_copy(c).start()

    groups = nfreq // GROUP
    prow = lax.broadcasted_iota(jnp.int32, (QUAD, 128), 0)
    pcol = lax.broadcasted_iota(jnp.int32, (QUAD, 128), 1)
    left = lax.broadcasted_iota(jnp.int32, (QUAD // 2, 128), 1) < QUAD

    def packed(whole):
        turned = pltpu.roll(whole, QUAD, 1)
        real = whole[:QUAD] + turned[QUAD:]
        imag = turned[:QUAD] - whole[QUAD:]
        mixed = jnp.where(prow <= pcol, real, imag)
        low = pltpu.roll(mixed[QUAD // 2 :], QUAD, 1)
        return jnp.where(left, mixed[: QUAD // 2], low).astype(jnp.bfloat16)

    shift, part, first, used = row_fields([starts_ref[b] for b in range(NBLK)])
    quarter = part * (NFFT // 4)
    scale = 0.5 / math.sqrt(0.375 * NFFT)
    lane = lax.broadcasted_iota(jnp.int32, (FREQ_ROWS, 128), 1)

    @pl.loop(0, nt // 128)
    def _(i):
        cols = pl.ds(pl.multiple_of(i * 128, 128), 128)
        t = lane + i * 128 - first
        inside = (t >= 0) & (t < NFFT) & used
        window = scale + scale * negative_cosine(t)
        weight[:, cols] = jnp.where(inside, -window, 0.0)

    @pl.loop(0, nfreq)
    def _(j):
        bins = freqs_ref[j] + (shift - HALF) * alpha_ref[0]
        base = pl.multiple_of(j * FREQ_ROWS, 16)
        turn = bins & 3
        even = jnp.where(turn == 0, 1.0, jnp.where(turn == 2, -1.0, 0.0))
        odd = jnp.where(turn == 1, 1.0, jnp.where(turn == 3, -1.0, 0.0))
        step = bins * (lane - first) + quarter
        here = negative_cosine(step)
        ahead = negative_cosine(step + NFFT // 4)

        def column(i, carry):
            here, ahead = carry
            cols = pl.ds(pl.multiple_of(i * 128, 128), 128)
            value = here * weight[:, cols]
            table[pl.ds(base, FREQ_ROWS), cols] = value.astype(jnp.bfloat16)
            return here * even + ahead * odd, ahead * even - here * odd

        lax.fori_loop(0, nt // 128, column, (here, ahead))

    def far_first(step, count):
        return lax.rem(step + lax.div(me * count, n) + count // 2, count)

    def table_rows(g):
        return pl.ds(pl.multiple_of(g * (GROUP * FREQ_ROWS), 16), GROUP * FREQ_ROWS)

    def correlate(c, g, result):
        result = result.astype(jnp.bfloat16)
        for i in range(GROUP):
            j = g * GROUP + i
            lines = result[i * FREQ_ROWS : i * FREQ_ROWS + GRAM_ROWS]
            own = i * FREQ_ROWS + GRAM_ROWS
            stage[c, j] = result[own : own + 2 * NBLK].reshape(NBLK, 2, width)
            product = lax.dot_general(
                lines, lines, (((1,), (1,)), ((), ())), preferred_element_type=jnp.float32
            )
            if c > 0:
                product += accum[j]
            if c == nchunk - 1:
                pack_out[j] = packed(product)
            else:
                accum[j] = product

    def send_spectra(c):
        @pl.loop(0, n - 1)
        def _(k):
            spec_copy(c, peer_at(k), me).start()

        own_spec_copy(c).start()

    for c in range(nchunk - 1):
        own_copy(c).wait()

        @pl.loop(1, n)
        def _(k):
            peer = lax.rem(me + k, n)
            raw_copy(c, peer, peer).wait_recv()

        @pl.loop(0, groups)
        def _(g):
            result = jnp.dot(
                table[table_rows(g), :], slabs[c][...], preferred_element_type=jnp.float32
            )
            correlate(c, g, result)

        send_spectra(c)

    c = nchunk - 1
    sources = n // PARTS
    for q in range(PARTS):
        part_index = far_first(q, PARTS)

        @pl.loop(0, sources)
        def _(i):
            peer = part_index * sources + i

            @pl.when(peer != me)
            def _():
                raw_copy(c, peer, peer).wait_recv()

            @pl.when(peer == me)
            def _():
                own_copy(c).wait()

        span = pl.ds(pl.multiple_of(part_index * (nt // PARTS), 128), nt // PARTS)

        @pl.loop(0, groups)
        def _(step):
            g = far_first(step, groups)
            result = jnp.dot(
                table[table_rows(g), span], slabs[c][span, :], preferred_element_type=jnp.float32
            )
            if q > 0:
                result += sums[table_rows(g), :]
            if q < PARTS - 1:
                sums[table_rows(g), :] = result
            else:
                correlate(c, g, result)
                for i in range(GROUP):
                    j = g * GROUP + i

                    @pl.when(j != me)
                    def _():
                        gram_copy(j, me).start()

    send_spectra(c)

    pack_in[me] = pack_out[me]

    @pl.loop(1, n)
    def _(k):
        peer = lax.rem(me + k, n)
        gram_copy(peer, peer).wait_recv()

    total = pack_in[0].astype(jnp.float32)
    for p in range(1, n):
        total += pack_in[p].astype(jnp.float32)
    space_parts[my_space] = total

    @pl.loop(1, ns)
    def _(k):
        space_copy(lax.rem(my_space + k, ns), my_space).start()

    @pl.loop(1, ns)
    def _(k):
        peer = lax.rem(my_space + k, ns)
        pltpu.make_async_remote_copy(
            src_ref=space_parts.at[my_space],
            dst_ref=space_parts.at[peer],
            send_sem=space_send.at[peer],
            recv_sem=space_recv.at[peer],
            device_id=at_space(peer),
            device_id_type=MESH,
        ).wait_recv()

    total = space_parts[0]
    for p in range(1, ns):
        total += space_parts[p]
    total = total * (1.0 / total_cells)
    mixed = jnp.concatenate(
        [total, pltpu.roll(total, QUAD, 1), jnp.zeros((QUAD, 128), jnp.float32)], axis=0
    )
    flipped = mixed.T[:QUAD]
    mixed = mixed[:QUAD]
    real = jnp.where(prow <= pcol, mixed, flipped)
    imag = jnp.where(prow > pcol, mixed, jnp.where(prow == pcol, 0.0, -flipped))
    gram_ref[0, :, 0] = real[:ORDER, :ORDER]
    gram_ref[0, :, 1] = imag[:ORDER, :ORDER]

    for c in range(nchunk):
        own_spec_copy(c).wait()

        @pl.loop(1, n)
        def _(k):
            peer = lax.rem(me + k, n)
            spec_copy(c, peer, peer).wait_recv()

    for c in range(nchunk):

        @pl.loop(1, n)
        def _(k):
            peer = lax.rem(me + k, n)
            raw_copy(c, peer, me).wait_send()
            spec_copy(c, peer, me).wait_send()

    @pl.loop(1, n)
    def _(k):
        peer = lax.rem(me + k, n)
        gram_copy(peer, me).wait_send()

    @pl.loop(1, ns)
    def _(k):
        space_copy(lax.rem(my_space + k, ns), my_space).wait_send()


def solution(mesh):
    n = mesh.shape["freq"]
    ns = mesh.shape["space"]

    def per_device(series, starts, freqs, alpha):
        rows, slab_cells = series.shape
        nfreq = freqs.shape[0]
        nt = rows * n
        own_cells = slab_cells // n
        nchunk = max(2, own_cells // 256)
        width = own_cells // nchunk
        smem = pl.BlockSpec(memory_space=pltpu.SMEM)
        table_rows = nfreq * FREQ_ROWS
        cost = pl.CostEstimate(
            flops=2 * table_rows * nt * own_cells,
            bytes_accessed=2 * rows * slab_cells * 2,
            transcendentals=0,
        )
        dma = pltpu.SemaphoreType.DMA
        spec, gram = pl.pallas_call(
            functools.partial(kernel, n, ns, nfreq, nchunk, slab_cells * ns),
            out_shape=(
                jax.ShapeDtypeStruct((NBLK, 2, slab_cells), jnp.bfloat16),
                jax.ShapeDtypeStruct((1, ORDER, 2, ORDER), jnp.float32),
            ),
            in_specs=[smem, smem, smem, pl.BlockSpec(memory_space=pl.ANY)],
            out_specs=(
                pl.BlockSpec(memory_space=pl.ANY),
                pl.BlockSpec(memory_space=pltpu.VMEM),
            ),
            scratch_shapes=[
                pltpu.VMEM((table_rows, nt), jnp.bfloat16),
                pltpu.VMEM((FREQ_ROWS, nt), jnp.float32),
                pltpu.VMEM((nchunk, nfreq, NBLK, 2, width), jnp.bfloat16),
                pltpu.VMEM((nchunk, n, rows, width), jnp.bfloat16),
                pltpu.VMEM((table_rows, width), jnp.float32),
                pltpu.VMEM((nfreq, GRAM_ROWS, GRAM_ROWS), jnp.float32),
                pltpu.VMEM((nfreq, QUAD // 2, 128), jnp.bfloat16),
                pltpu.VMEM((n, QUAD // 2, 128), jnp.bfloat16),
                pltpu.VMEM((ns, QUAD // 2, 128), jnp.float32),
                dma((nchunk, n)),
                dma((nchunk, n)),
                dma((nchunk, n)),
                dma((nchunk, n)),
                dma((n,)),
                dma((n,)),
                dma((ns,)),
                dma((ns,)),
                dma((2, nchunk)),
                dma((nchunk, n)),
            ]
            + [pltpu.VMEM((nt, width), jnp.bfloat16)] * nchunk,
            compiler_params=pltpu.CompilerParams(
                collective_id=0, has_side_effects=True, vmem_limit_bytes=60 * 1024 * 1024
            ),
            cost_estimate=cost,
        )(starts, freqs, alpha, series)
        own = jnp.transpose(spec, (1, 0, 2))
        return own[None], jnp.transpose(gram, (0, 2, 1, 3))

    placed = (P("freq", "space"), P(), P(), P())
    return jax.shard_map(
        per_device,
        mesh=mesh,
        in_specs=placed,
        out_specs=(P("freq", None, None, "space"), P("freq", None, None, None)),
        check_vma=False,
    )
```
